256 devices in a mesh: seq: 64 (over z, x, core), head: 4 (over y).
Axes of the slice: x: 4, y: 4, z: 8, core: 2. Of those that a mesh axis runs over, the one named last changes fastest.
Arguments:
- hidden_in: bfloat16 [65536, 2048], P('seq', 'head'), may hold values from -16 to 16
- value_weight: bfloat16 [2048, 2048], P(None, 'head'), may hold values from -0.125 to 0.125
- queries: bfloat16 [65536, 2048], P('seq', 'head'), may hold values from -6 to 6
- keys: bfloat16 [65536, 2048], P('seq', 'head'), may hold values from -6 to 6
- level_weights: bfloat16 [17, 16, 65536], P(None, 'head', 'seq'), may hold values from 0 to 1
- out_grad: bfloat16 [65536, 2048], P('seq', 'head'), may hold values from -0.0234375 to 0.0234375
Outputs:
- attended: bfloat16 [65536, 2048], P('seq', 'head')
- weight_grad: float32 [2048, 2048], P('seq', 'head')
The draws below stay inside these ranges and needn't reach their ends.
All inputs are finite; a program needn't handle non-finite values.
Results may differ from the reference program's by a relative error of at most 0.0057.
Values may be sent and summed in bfloat16 or wider, within the bound.
No kernel may reach another device: no remote copies, remote signals or barrier semaphores. Data moves between devices by JAX's collectives and lax.ppermute only.
A program may use at most 128 MiB of HBM per device.

```python
import math
import jax
import jax.numpy as jnp
from jax import lax

D = 2048
H = 16
HD = 128
TOK_DEV = 1024
TOKENS = 65536
TOK_BITS = 10
SEQ_BITS = 6
LEVELS = 17
N_SEQ = 64


def draw_level_weights(key, part):
    level_axis = jnp.arange(LEVELS, dtype=jnp.float32)[:, None, None]
    spread = jnp.exp2(jnp.maximum(level_axis - 1.0, 0.0))
    base = jnp.exp(jax.random.uniform(key, (LEVELS, H, TOKENS), jnp.float32, math.log(0.1), math.log(2.0)))
    return (base / jnp.sqrt(HD * spread)).astype(jnp.bfloat16)


def strengthened(entries, stream_key, source, target, parts, factor):
    def block_of(dim):
        return (jnp.arange(entries.shape[dim]) // (entries.shape[dim] // parts)).reshape((-1,) + (1,) * (entries.ndim - 1 - dim))

    first = jax.random.permutation(stream_key, parts)[block_of(target)]
    far = (block_of(target) + parts // 2) % parts
    return jnp.where((block_of(source) == first) | (block_of(source) == far), factor * entries, entries)


def block_levels(own_key, dims, cuts, smallest, largest):
    level, own = 1.0, jax.random.fold_in(own_key, 6)
    for dim, blocks in cuts:
        steps = jnp.exp(jax.random.uniform(jax.random.fold_in(own, dim), (blocks,), jnp.float32, smallest / len(cuts), largest / len(cuts)))
        level = level * jnp.repeat(steps, dims[dim] // blocks).reshape([-1 if axis == dim else 1 for axis in range(len(dims))])
    return level


def normal_values(rng, shape, deviation, reach, cuts=(), kind=jnp.bfloat16):
    entries = deviation * jax.random.normal(rng, shape, jnp.float32)
    if cuts:
        entries = entries * block_levels(rng, shape, cuts, -0.22, 0.18)
    return jnp.clip(entries, -reach, reach).astype(kind)


def gaussian_with(stream_key, dims, scale, limit, cuts, heavy, kind=jnp.bfloat16):
    entries = scale * jax.random.normal(stream_key, dims, jnp.float32)
    if cuts:
        entries = entries * block_levels(stream_key, dims, cuts, -0.22, 0.18)
    return jnp.clip(strengthened(entries, jax.random.fold_in(stream_key, 3), *heavy), -limit, limit).astype(kind)


def setup_inputs(seed: int = 0) -> dict:
    seeds = jax.random.split(jax.random.key(seed), 7)
    return {
        "hidden_in": gaussian_with(seeds[0], (TOKENS, D), 1.0, 16.0, ((0, 64), (1, 4)), (0, 1, 64, 4.0)),
        "value_weight": normal_values(seeds[1], (D, H * HD), D ** -0.5, 0.125, ((1, 4),)),
        "queries": normal_values(seeds[2], (TOKENS, H * HD), 1.0, 6.0, ((0, 64), (1, 4))),
        "keys": normal_values(seeds[3], (TOKENS, H * HD), 1.0, 6.0, ((0, 64), (1, 4))),
        "level_weights": draw_level_weights(jax.random.fold_in(seeds[6], 71), 0),
        "out_grad": normal_values(seeds[5], (TOKENS, H * HD), (TOKENS ** -0.5), 0.0234375, ((0, 64), (1, 4))),
    }


def rounded_copy(array):
    return lax.optimization_barrier(array.astype(jnp.bfloat16)).astype(jnp.float32)


def level_of(later, earlier, depth):
    differ = jnp.bitwise_xor(later, earlier)
    result = jnp.zeros(differ.shape, jnp.int32)
    for digit in range(depth):
        result = result + (differ >= (1 << digit)).astype(jnp.int32)
    return result


def near_block(queries3, keys3, values3, grads3, near_weights, depth):
    length = queries3.shape[0]
    count = max(1, length // 512)
    span_rows = length // count
    pieces = []
    value_back = jnp.zeros(values3.shape, jnp.float32)
    for index in range(count):
        first = index * span_rows
        last = first + span_rows
        scores = jnp.einsum("thd,shd->hts", queries3[first:last].astype(jnp.float32),
                            keys3[:last].astype(jnp.float32), precision=lax.Precision.HIGHEST)
        later = first + jnp.arange(span_rows, dtype=jnp.int32)[:, None]
        earlier = jnp.arange(last, dtype=jnp.int32)[None, :]
        table = level_of(later, earlier, depth)
        weight = jnp.zeros(scores.shape, jnp.float32)
        for level_index in range(depth + 1):
            weight = weight + jnp.where(table == level_index, near_weights[level_index][:, first:last, None], 0.0)
        weight = jnp.where(earlier <= later, weight, 0.0)
        probs = rounded_copy(scores * weight)
        pieces.append(jnp.einsum("hts,she->the", probs, values3[:last].astype(jnp.float32),
                                 precision=lax.Precision.HIGHEST))
        value_back = value_back.at[:last].add(jnp.einsum("hts,the->she", probs, grads3[first:last].astype(jnp.float32),
                                                         precision=lax.Precision.HIGHEST))
    return jnp.concatenate(pieces, axis=0), value_back


def reference(hidden_in, value_weight, queries, keys, level_weights, out_grad):
    head_count = level_weights.shape[1]
    span_cols = value_weight.shape[1]
    head_width = span_cols // head_count
    values = jnp.dot(hidden_in, value_weight, preferred_element_type=jnp.float32).astype(jnp.bfloat16)
    shape_four = (N_SEQ, TOK_DEV, head_count, head_width)
    queries4 = queries.reshape(shape_four)
    keys4 = keys.reshape(shape_four)
    values4 = values.reshape(shape_four)
    grads4 = out_grad.reshape(shape_four)
    near_weights = level_weights[:TOK_BITS + 1].astype(jnp.float32).reshape(
        TOK_BITS + 1, head_count, N_SEQ, TOK_DEV).transpose(2, 0, 1, 3)
    far_weights = level_weights[TOK_BITS + 1:].astype(jnp.float32).reshape(
        SEQ_BITS, head_count, N_SEQ, TOK_DEV)

    def one_block(packed):
        return near_block(packed[0], packed[1], packed[2], packed[3], packed[4], TOK_BITS)

    attended, value_grad = lax.map(one_block, (queries4, keys4, values4, grads4, near_weights))
    queries_wide = queries4.astype(jnp.float32)
    keys_wide = keys4.astype(jnp.float32)
    key_state = jnp.einsum("bthd,bthe->bhde", keys_wide, values4.astype(jnp.float32),
                           precision=lax.Precision.HIGHEST)
    block_index = jnp.arange(N_SEQ, dtype=jnp.int32)
    for digit in range(SEQ_BITS):
        group_size = 1 << digit
        group_count = N_SEQ // group_size
        group_of = block_index >> digit
        upper = (group_of & 1) == 1
        grouped = key_state.reshape(group_count, group_size, head_count, head_width, head_width).sum(axis=1)
        chosen = grouped[jnp.maximum(group_of - 1, 0)]
        far_state = jnp.where(upper[:, None, None, None], chosen, 0.0)
        level_scale = far_weights[digit].transpose(1, 2, 0)[:, :, :, None]
        product = jnp.einsum("bthd,bhde->bthe", queries_wide, rounded_copy(far_state),
                             precision=lax.Precision.HIGHEST)
        attended = attended + product * level_scale
        weighted = rounded_copy(queries_wide * level_scale)
        query_state = jnp.einsum("bthd,bthe->bhde", weighted, grads4.astype(jnp.float32),
                                 precision=lax.Precision.HIGHEST)
        grouped_back = query_state.reshape(group_count, group_size, head_count, head_width, head_width).sum(axis=1)
        chosen_back = grouped_back[jnp.minimum(group_of + 1, group_count - 1)]
        back_state = jnp.where(upper[:, None, None, None], 0.0, chosen_back)
        value_grad = value_grad + jnp.einsum("bshd,bhde->bshe", keys_wide, rounded_copy(back_state),
                                             precision=lax.Precision.HIGHEST)
    attended_out = attended.astype(jnp.bfloat16).reshape(TOKENS, span_cols)
    value_flat = value_grad.astype(jnp.bfloat16).reshape(TOKENS, span_cols)
    weight_grad = lax.dot_general(hidden_in, value_flat, (((0,), (0,)), ((), ())),
                                  preferred_element_type=jnp.float32)
    return attended_out, weight_grad
```

```python
import functools

import jax
import jax.numpy as jnp
from jax import lax
from jax.experimental import pallas as pl
from jax.experimental.pallas import tpu as pltpu
from jax.sharding import Mesh, PartitionSpec as P

BF = jnp.bfloat16
F32 = jnp.float32
HW = 128
NH = 4
TOK = 1024
BLK = 256
DEPTH = 10
FAR = 6
PART = 512
NX, NZ = 4, 8
VMEM = 56 * 1024 * 1024

NT = (((1,), (1,)), ((), ()))
TN = (((0,), (0,)), ((), ()))
NN = (((1,), (0,)), ((), ()))


def dot(a, b, dims=NN):
    return lax.dot_general(a, b, dims, preferred_element_type=F32)


def shift(value, axis, distance, size):
    return lax.ppermute(value, axis, [(i, (i + distance) % size) for i in range(size)])


def swap(value, axis, distance, size):
    return lax.ppermute(value, axis, [(i, i ^ distance) for i in range(size)])


def params():
    return pltpu.CompilerParams(
        dimension_semantics=("arbitrary",), vmem_limit_bytes=VMEM
    )


def cost(flops, moved):
    return pl.CostEstimate(flops=int(flops), bytes_accessed=int(moved), transcendentals=0)


def query_state_kernel(place, q_ref, g_ref, lw_ref, first_ref, send_ref, keep_ref, stack):
    slot = pl.program_id(0)
    turned = q_ref[...].astype(F32).T
    for digit in range(FAR):
        row = lw_ref[0, DEPTH + 1 + digit : DEPTH + 2 + digit, :]
        stack[digit * HW : (digit + 1) * HW, :] = (turned * row).astype(BF)
    state = dot(stack[...], g_ref[...])
    first_ref[0] = state[:HW]
    rest = state[HW:].reshape(FAR - 1, HW, HW)

    @pl.when(slot < 2)
    def _():
        send_ref[0] = rest

    @pl.when(slot >= 2)
    def _():
        keep_ref[0] = rest


def query_states(place, queries, out_grad, weights):
    def head(s, place):
        return lax.rem(2 * (1 - place[0]) + s, NH)

    return pl.pallas_call(
        query_state_kernel,
        grid_spec=pltpu.PrefetchScalarGridSpec(
            num_scalar_prefetch=1,
            grid=(NH,),
            in_specs=[
                pl.BlockSpec((TOK, HW), lambda s, p: (0, head(s, p))),
                pl.BlockSpec((TOK, HW), lambda s, p: (0, head(s, p))),
                pl.BlockSpec((1, DEPTH + 1 + FAR, TOK), lambda s, p: (head(s, p), 0, 0)),
            ],
            out_specs=[
                pl.BlockSpec((1, HW, HW), lambda s, p: (s, 0, 0)),
                pl.BlockSpec((1, FAR - 1, HW, HW), lambda s, p: (jnp.minimum(s, 1), 0, 0, 0)),
                pl.BlockSpec((1, FAR - 1, HW, HW), lambda s, p: (jnp.maximum(s - 2, 0), 0, 0, 0)),
            ],
            scratch_shapes=[pltpu.VMEM((FAR * HW, TOK), BF)],
        ),
        out_shape=[
            jax.ShapeDtypeStruct((NH, HW, HW), F32),
            jax.ShapeDtypeStruct((2, FAR - 1, HW, HW), F32),
            jax.ShapeDtypeStruct((2, FAR - 1, HW, HW), F32),
        ],
        compiler_params=params(),
        cost_estimate=cost(2e9, 4e6),
        name="query_states",
    )(place, queries, out_grad, weights)


def differing():
    earlier = lax.broadcasted_iota(jnp.int32, (BLK, BLK), 0)
    later = lax.broadcasted_iota(jnp.int32, (BLK, BLK), 1)
    return earlier ^ later, earlier <= later


def near_square(k_ref, q_ref, lw_ref, high, low, differ, causal):
    scores = dot(
        k_ref[low * BLK : (low + 1) * BLK, :], q_ref[high * BLK : (high + 1) * BLK, :], NT
    )
    columns = slice(high * BLK, (high + 1) * BLK)
    if low != high:
        level = BLK.bit_length() + (high ^ low).bit_length() - 1
        weight = lw_ref[0, level : level + 1, columns]
    else:
        weight = jnp.broadcast_to(lw_ref[0, 0:1, columns], (BLK, BLK))
        for level in range(1, BLK.bit_length()):
            row = lw_ref[0, level : level + 1, columns]
            weight = jnp.where(differ >= 1 << (level - 1), row, weight)
        weight = jnp.where(causal, weight, 0.0)
    return (scores * weight).astype(BF)


def near_back_kernel(q_ref, k_ref, g_ref, lw_ref, back_ref):
    differ, causal = differing()
    for low in range(TOK // BLK):
        total = None
        for high in range(low, TOK // BLK):
            square = near_square(k_ref, q_ref, lw_ref, high, low, differ, causal)
            term = dot(square, g_ref[high * BLK : (high + 1) * BLK, :])
            total = term if total is None else total + term
        back_ref[low * BLK : (low + 1) * BLK, :] = total


def near_ahead_kernel(q_ref, k_ref, v_ref, lw_ref, ahead_ref):
    differ, causal = differing()
    for high in range(TOK // BLK):
        total = None
        for low in range(high + 1):
            square = near_square(k_ref, q_ref, lw_ref, high, low, differ, causal)
            term = dot(v_ref[low * BLK : (low + 1) * BLK, :], square, TN)
            total = term if total is None else total + term
        ahead_ref[0, :, high * BLK : (high + 1) * BLK] = total


def of_head():
    return pl.BlockSpec((TOK, HW), lambda h: (0, h))


def lw_of_head():
    return pl.BlockSpec((1, DEPTH + 1 + FAR, TOK), lambda h: (h, 0, 0))


def near_back(queries, keys, out_grad, weights):
    return pl.pallas_call(
        near_back_kernel,
        grid=(NH,),
        in_specs=[of_head(), of_head(), of_head(), lw_of_head()],
        out_specs=of_head(),
        out_shape=jax.ShapeDtypeStruct((TOK, NH * HW), F32),
        compiler_params=params(),
        cost_estimate=cost(4e9, 5e6),
        name="near_back",
    )(queries, keys, out_grad, weights)


def near_ahead(queries, keys, values, weights):
    return pl.pallas_call(
        near_ahead_kernel,
        grid=(NH,),
        in_specs=[of_head(), of_head(), of_head(), lw_of_head()],
        out_specs=pl.BlockSpec((1, HW, TOK), lambda h: (h, 0, 0)),
        out_shape=jax.ShapeDtypeStruct((NH, HW, TOK), F32),
        compiler_params=params(),
        cost_estimate=cost(4e9, 5e6),
        name="near_ahead",
    )(queries, keys, values, weights)


def values_kernel(place, own, lu, ll, ru, rl, fu, fl, w_ref, k_ref, v_ref, state_ref):
    tile = pl.program_id(0)
    core, me = place[0], place[1]
    upper = tile < 2

    def rows(part):
        at = pl.multiple_of(lax.rem(part, 4) * PART, PART)
        return w_ref[pl.ds(at, PART), :]

    total = dot(own[...], rows(me))
    for distance, (top, bottom) in ((3, (lu, ll)), (1, (ru, rl)), (2, (fu, fl))):
        part = jnp.where(upper, top[...], bottom[...])
        total = total + dot(part, rows(me + distance))
    v_ref[...] = total.astype(BF)

    @pl.when(tile == 0)
    def _():
        state_ref[...] = jnp.zeros_like(state_ref)

    for slot in range(NH):
        at = pl.multiple_of(lax.rem(2 * (1 - core) + slot, NH) * HW, HW)
        state_ref[slot] += dot(k_ref[:, pl.ds(at, HW)], v_ref[:, pl.ds(at, HW)], TN)


def values_and_states(place, parts, value_weight, keys):
    tile = pl.BlockSpec((BLK, PART), lambda i, p: (i, 0))
    top = pl.BlockSpec((BLK, PART), lambda i, p: (jnp.minimum(i, 1), 0))
    bottom = pl.BlockSpec((BLK, PART), lambda i, p: (jnp.maximum(i - 2, 0), 0))
    return pl.pallas_call(
        values_kernel,
        grid_spec=pltpu.PrefetchScalarGridSpec(
            num_scalar_prefetch=1,
            grid=(TOK // BLK,),
            in_specs=[
                tile,
                top,
                bottom,
                top,
                bottom,
                top,
                bottom,
                pl.BlockSpec((4 * PART, NH * HW), lambda i, p: (0, 0)),
                pl.BlockSpec((BLK, NH * HW), lambda i, p: (i, 0)),
            ],
            out_specs=[
                pl.BlockSpec((BLK, NH * HW), lambda i, p: (i, 0)),
                pl.BlockSpec((NH, HW, HW), lambda i, p: (0, 0, 0)),
            ],
        ),
        out_shape=[
            jax.ShapeDtypeStruct((TOK, NH * HW), BF),
            jax.ShapeDtypeStruct((NH, HW, HW), F32),
        ],
        compiler_params=params(),
        cost_estimate=cost(3e9, 8e6),
        name="values_and_states",
    )(place, *parts, value_weight, keys)


def weight_kernel(place, near_ref, k_ref, mine_ref, other_ref, own, lu, ll, ru, rl, fu, fl, send_ref, keep_ref, grad, term):
    step = pl.program_id(0)
    core, me, col = place[0], place[1], place[2]
    half = TOK // 2

    @pl.when(step == 0)
    def _():
        for slot in range(NH):
            at = pl.multiple_of(lax.rem(2 * core + slot, NH) * HW, HW)
            state = mine_ref[slot] if slot < 2 else other_ref[slot - 2]
            far = dot(k_ref[:, pl.ds(at, HW)], state)
            grad[:, pl.ds(at, HW)] = (near_ref[:, pl.ds(at, HW)] + far).astype(BF)
        term[...] = dot(own[...], grad[...], TN)

    for index, (top, bottom) in ((1, (lu, ll)), (2, (ru, rl)), (3, (fu, fl))):

        @pl.when(step == index)
        def _(top=top, bottom=bottom):
            term[...] = dot(top[...], grad[:half, :], TN) + dot(bottom[...], grad[half:, :], TN)

    distance = jnp.where(step == 0, 0, jnp.where(step == 1, 3, jnp.where(step == 2, 1, 2)))
    part = lax.rem(me + distance, 4)
    for plane in range(2):
        for x in range(NX):
            turn = lax.rem(x - col + NX, NX)
            at = plane * 256 + x * 64
            send_ref[turn, 2 * part + plane] = term[pl.ds(pl.multiple_of(at + (1 - core) * 32, 32), 32), :]
            keep_ref[turn, 2 * part + plane] = term[pl.ds(pl.multiple_of(at + core * 32, 32), 32), :]


def weight_terms(place, near, keys, mine, other, parts):
    whole = lambda *shape: pl.BlockSpec(shape, lambda i, p: (0,) * len(shape))
    half = TOK // 2
    return pl.pallas_call(
        weight_kernel,
        grid_spec=pltpu.PrefetchScalarGridSpec(
            num_scalar_prefetch=1,
            grid=(4,),
            in_specs=[
                whole(TOK, NH * HW),
                whole(TOK, NH * HW),
                whole(2, HW, HW),
                whole(2, HW, HW),
                whole(TOK, PART),
            ]
            + [whole(half, PART)] * 6,
            out_specs=[whole(NX, NZ, 32, NH * HW), whole(NX, NZ, 32, NH * HW)],
            scratch_shapes=[pltpu.VMEM((TOK, NH * HW), BF), pltpu.VMEM((PART, NH * HW), F32)],
        ),
        out_shape=[jax.ShapeDtypeStruct((NX, NZ, 32, NH * HW), F32)] * 2,
        compiler_params=params(),
        cost_estimate=cost(4e9, 12e6),
        name="weight_terms",
    )(place, near, keys, mine, other, *parts)


def attended_kernel(place, q_ref, lw_ref, near_ref, first_ref, far_ref, out_ref, stack):
    stack[:HW, :] = first_ref[0].astype(F32).T.astype(BF)
    for digit in range(1, FAR):
        stack[digit * HW : (digit + 1) * HW, :] = far_ref[0, digit - 1].astype(F32).T.astype(BF)
    product = dot(stack[...], q_ref[...], NT)
    total = near_ref[0]
    for digit in range(FAR):
        row = lw_ref[0, DEPTH + 1 + digit : DEPTH + 2 + digit, :]
        total = total + product[digit * HW : (digit + 1) * HW, :] * row
    out_ref[...] = total.T.astype(BF)


def attend(place, queries, weights, near, first, far):
    def head(s, p):
        return lax.rem(2 * p[0] + s, NH)

    return pl.pallas_call(
        attended_kernel,
        grid_spec=pltpu.PrefetchScalarGridSpec(
            num_scalar_prefetch=1,
            grid=(NH,),
            in_specs=[
                pl.BlockSpec((TOK, HW), lambda s, p: (0, head(s, p))),
                pl.BlockSpec((1, DEPTH + 1 + FAR, TOK), lambda s, p: (head(s, p), 0, 0)),
                pl.BlockSpec((1, HW, TOK), lambda s, p: (head(s, p), 0, 0)),
                pl.BlockSpec((1, HW, HW), lambda s, p: (s, 0, 0)),
                pl.BlockSpec((1, FAR - 1, HW, HW), lambda s, p: (s, 0, 0, 0)),
            ],
            out_specs=pl.BlockSpec((TOK, HW), lambda s, p: (0, head(s, p))),
            scratch_shapes=[pltpu.VMEM((FAR * HW, HW), BF)],
        ),
        out_shape=jax.ShapeDtypeStruct((TOK, NH * HW), BF),
        compiler_params=params(),
        cost_estimate=cost(2e9, 5e6),
        name="attended",
    )(place, queries, weights, near, first, far)


def back_sums(first, send, keep, x, z):
    first_got = lax.ppermute(first, "core", [(1, 0)])
    pairs = keep + swap(send, "core", 1, 2)
    pending = pairs[:, 2:]
    got = swap(pending.astype(BF), "z", 1, NZ).astype(F32)
    total = jnp.where(z & 1 == 0, got[:, 0], 0.0)
    pending = pending[:, 1:] + got[:, 1:]
    got = swap(pending.astype(BF), "z", 2, NZ).astype(F32)
    total = total + jnp.where(z & 2 == 0, got[:, 0], 0.0)
    pending = pending[:, 1] + got[:, 1]
    total = total + lax.ppermute(pending.astype(BF), "z", [(i + 4, i) for i in range(4)]).astype(F32)
    summed = total
    for distance in (1, 3, 2):
        to = (x + distance) % NX
        level = jnp.where(to ^ x == 1, pairs[:, 0], pairs[:, 1])
        message = total + jnp.where(to < x, level, 0.0)
        summed = summed + shift(message.astype(BF), "x", distance, NX).astype(F32)
    other = swap(summed, "core", 1, 2)
    return (summed + first_got[:2]).astype(BF), (other + first_got[2:]).astype(BF)


def far_states(state, core, x, z):
    got = swap(state, "core", 1, 2)
    first = jnp.where(core == 1, got, 0.0).astype(BF)
    pair = state[2:] + got[:2]
    left, far, right = (shift(pair.astype(BF), "x", d, NX).astype(F32) for d in (1, 2, 3))
    levels = [
        jnp.where(x & 1 == 1, left, 0.0),
        jnp.where(x == 2, left + far, jnp.where(x == 3, far + right, 0.0)),
    ]
    running = pair + left + far + right
    got = swap(running.astype(BF), "z", 1, NZ).astype(F32)
    levels.append(jnp.where(z & 1 == 1, got, 0.0))
    running = running + got
    got = swap(running.astype(BF), "z", 2, NZ).astype(F32)
    levels.append(jnp.where(z & 2 == 2, got, 0.0))
    running = running + got
    levels.append(lax.ppermute(running.astype(BF), "z", [(i, i + 4) for i in range(4)]).astype(F32))
    mine = jnp.stack([level.astype(BF) for level in levels], axis=1)
    other = swap(mine, "core", 1, 2)
    return first, jnp.concatenate([mine, other], axis=0)


def local(hidden_in, value_weight, queries, keys, level_weights, out_grad):
    z, x, core, me = (lax.axis_index(a) for a in ("z", "x", "core", "head"))
    place = jnp.stack([core, me, x]).astype(jnp.int32)
    weights = level_weights.astype(F32).transpose(1, 0, 2)

    half = TOK // 2
    upper, lower = hidden_in[:half], hidden_in[half:]
    lu = shift(upper, "head", 1, 4)
    rl = shift(lower, "head", 3, 4)
    ll = shift(lower, "head", 1, 4)
    ru = shift(upper, "head", 3, 4)
    fu = shift(lu, "head", 1, 4)
    fl = shift(rl, "head", 3, 4)
    parts = (hidden_in, lu, ll, ru, rl, fu, fl)

    first, send, keep = query_states(place, queries, out_grad, weights)
    mine, other = back_sums(first, send, keep, x, z)
    back = near_back(queries, keys, out_grad, weights)

    values, state = values_and_states(place, parts, value_weight, keys)
    send, keep = weight_terms(place, back, keys, mine, other, parts)

    zero, rest = far_states(state, core, x, z)
    ahead = near_ahead(queries, keys, values, weights)

    summed = keep + swap(send, "core", 1, 2)
    rows = summed[0]
    for distance in (1, 3, 2):
        rows = rows + shift(summed[distance].astype(BF), "x", distance, NX).astype(F32)
    got = lax.all_to_all(rows.astype(BF), "z", 0, 0, tiled=True)
    weight_grad = got.astype(F32).sum(axis=0)

    attended = attend(place, queries, weights, ahead, zero, rest)
    return attended, weight_grad


def solution(mesh):
    fine = Mesh(mesh.devices.reshape(NZ, NX, 2, 4), ("z", "x", "core", "head"))
    seq = ("z", "x", "core")
    return jax.shard_map(
        local,
        mesh=fine,
        in_specs=(
            P(seq, "head"),
            P(None, "head"),
            P(seq, "head"),
            P(seq, "head"),
            P(None, "head", seq),
            P(seq, "head"),
        ),
        out_specs=(P(seq, "head"), P(seq, "head")),
        check_vma=False,
    )
```

```python
import functools

import jax
import jax.numpy as jnp
from jax import lax
from jax.experimental import pallas as pl
from jax.experimental.pallas import tpu as pltpu
from jax.sharding import Mesh, PartitionSpec as P

BF = jnp.bfloat16
F32 = jnp.float32
HW = 128
NH = 4
TOK = 1024
BLK = 256
DEPTH = 10
FAR = 6
PART = 512
NX, NZ = 4, 8
VMEM = 24 * 1024 * 1024

NT = (((1,), (1,)), ((), ()))
TN = (((0,), (0,)), ((), ()))
NN = (((1,), (0,)), ((), ()))


def dot(a, b, dims=NN):
    return lax.dot_general(a, b, dims, preferred_element_type=F32)


def shift(value, axis, distance, size):
    return lax.ppermute(value, axis, [(i, (i + distance) % size) for i in range(size)])


def swap(value, axis, distance, size):
    return lax.ppermute(value, axis, [(i, i ^ distance) for i in range(size)])


def rows_of(lw_ref, first, count, head):
    rows = []
    for level in range(first, first + count):
        every = lw_ref[level].astype(F32)
        index = lax.broadcasted_iota(jnp.int32, every.shape, 0)
        rows.append(jnp.sum(jnp.where(index == head, every, 0.0), axis=0, keepdims=True))
    return rows


def whole(*shape):
    return pl.BlockSpec(shape, lambda *_: (0,) * len(shape))


LEVELS = whole(DEPTH + 1 + FAR, NH, TOK)


def params():
    return pltpu.CompilerParams(
        dimension_semantics=("arbitrary",), vmem_limit_bytes=VMEM
    )


def cost(us):
    return pl.CostEstimate(flops=int(us * 1.15e9), bytes_accessed=1000, transcendentals=0)


ANY = pl.BlockSpec(memory_space=pl.ANY)


def streamed(*values):
    return [pltpu.with_memory_space_constraint(value, pltpu.HBM) for value in values]


def turn_kernel(in_ref, *rest):
    turned = in_ref[...].T
    at = 0
    for out_ref in rest[1:]:
        out_ref[...] = turned[at : at + out_ref.shape[0], :]
        at += out_ref.shape[0]


def turned(value, side, count, name, after):
    rows, columns = value.shape
    part = columns // count
    return pl.pallas_call(
        turn_kernel,
        grid=(rows // side,),
        in_specs=[pl.BlockSpec((side, columns), lambda i: (i, 0)), ANY],
        out_specs=[pl.BlockSpec((part, side), lambda i: (0, i))] * count,
        out_shape=[jax.ShapeDtypeStruct((part, rows), value.dtype)] * count,
        compiler_params=params(),
        cost_estimate=cost(1.5),
        name=name,
    )(value, after)


def query_state_kernel(place, q_u, q_l, g_u, g_l, lw_ref, *rest):
    first_ref, send_ref, keep_ref, turned_ref, stack = rest[-5:]
    slot = pl.program_id(0)
    half = TOK // 2
    turned_ref[0, :, :half] = q_u[...].T
    turned_ref[0, :, half:] = q_l[...].T
    turned = turned_ref[0]
    head = lax.rem(2 * (1 - place[0]) + slot, NH)
    for digit, row in enumerate(rows_of(lw_ref, DEPTH + 1, FAR, head)):
        stack[digit * HW : (digit + 1) * HW, :] = turned * row.astype(BF)
    state = dot(stack[:, :half], g_u[...]) + dot(stack[:, half:], g_l[...])
    first_ref[0] = state[:HW]
    rest = state[HW:].reshape(FAR - 1, HW, HW)

    @pl.when(slot < 2)
    def _():
        send_ref[:, 0] = rest

    @pl.when(slot >= 2)
    def _():
        keep_ref[:, 0] = rest


def query_states(place, queries, out_grad, weights, *after):
    def head(s, place):
        return lax.rem(2 * (1 - place[0]) + s, NH)

    return pl.pallas_call(
        query_state_kernel,
        grid_spec=pltpu.PrefetchScalarGridSpec(
            num_scalar_prefetch=1,
            grid=(NH,),
            in_specs=[
                pl.BlockSpec((TOK // 2, HW), lambda s, p: (0, head(s, p))),
                pl.BlockSpec((TOK // 2, HW), lambda s, p: (1, head(s, p))),
                pl.BlockSpec((TOK // 2, HW), lambda s, p: (0, head(s, p))),
                pl.BlockSpec((TOK // 2, HW), lambda s, p: (1, head(s, p))),
                LEVELS,
            ]
            + [ANY] * len(after),
            out_specs=[
                pl.BlockSpec((1, HW, HW), lambda s, p: (s, 0, 0)),
                pl.BlockSpec((FAR - 1, 1, HW, HW), lambda s, p: (0, jnp.minimum(s, 1), 0, 0)),
                pl.BlockSpec((FAR - 1, 1, HW, HW), lambda s, p: (0, jnp.maximum(s - 2, 0), 0, 0)),
                pl.BlockSpec((1, HW, TOK), lambda s, p: (head(s, p), 0, 0)),
            ],
            scratch_shapes=[pltpu.VMEM((FAR * HW, TOK), BF)],
        ),
        out_shape=[
            jax.ShapeDtypeStruct((NH, HW, HW), F32),
            jax.ShapeDtypeStruct((FAR - 1, 2, HW, HW), F32),
            jax.ShapeDtypeStruct((FAR - 1, 2, HW, HW), F32),
            pltpu.HBM((NH, HW, TOK), BF),
        ],
        compiler_params=params(),
        cost_estimate=cost(4),
        name="query_states",
    )(place, *streamed(queries, queries, out_grad, out_grad, weights), *after)


SIDES = TOK // BLK
SQUARES = [(low, high) for low in range(SIDES) for high in range(low, SIDES)]


def diagonal(levels, start, differ, causal):
    columns = slice(start, start + HW)
    weight = jnp.broadcast_to(levels[0][:, columns], (HW, HW))
    for level in range(1, HW.bit_length()):
        weight = jnp.where(differ >= 1 << (level - 1), levels[level][:, columns], weight)
    return jnp.where(causal, weight, 0.0)


def near_kernel(base, k_ref, turned_ref, g_ref, lw_ref, *rest):
    back_ref, *near_refs = rest[-3:]
    levels = rows_of(lw_ref, 0, DEPTH + 1, base + pl.program_id(0))
    earlier = lax.broadcasted_iota(jnp.int32, (HW, HW), 0)
    later = lax.broadcasted_iota(jnp.int32, (HW, HW), 1)
    differ, causal = earlier ^ later, earlier <= later
    zero = jnp.zeros((HW, HW), BF)
    middle = HW.bit_length()
    total = None
    for index, (low, high) in enumerate(SQUARES):
        columns = slice(high * BLK, (high + 1) * BLK)
        scores = dot(k_ref[low * BLK : (low + 1) * BLK, :], turned_ref[0, :, columns])
        if low != high:
            level = BLK.bit_length() + (high ^ low).bit_length() - 1
            square = (scores * levels[level][:, columns]).astype(BF)
        else:
            start = high * BLK
            across = levels[middle][:, start + HW : start + BLK]
            upper = scores[:HW, :HW] * diagonal(levels, start, differ, causal)
            lower = scores[HW:, HW:] * diagonal(levels, start + HW, differ, causal)
            top = jnp.concatenate([upper, scores[:HW, HW:] * across], axis=1).astype(BF)
            square = jnp.concatenate(
                [top, jnp.concatenate([zero, lower.astype(BF)], axis=1)], axis=0
            )
        near_refs[index // 5][0, index % 5] = square
        term = dot(square, g_ref[columns, :])
        total = term if low == high else total + term
        if high == SIDES - 1:
            back_ref[low * BLK : (low + 1) * BLK, :] = total


def near(base, keys, turned, out_grad, weights, *after):
    head = pl.BlockSpec((TOK, HW), lambda h: (0, base + h))
    return pl.pallas_call(
        functools.partial(near_kernel, base),
        grid=(2,),
        in_specs=[head, pl.BlockSpec((1, HW, TOK), lambda h: (base + h, 0, 0)), head, LEVELS]
        + [ANY] * len(after),
        out_specs=[
            pl.BlockSpec((TOK, HW), lambda h: (0, h)),
            pl.BlockSpec((1, 5, BLK, BLK), lambda h: (h, 0, 0, 0)),
            pl.BlockSpec((1, 5, BLK, BLK), lambda h: (h, 0, 0, 0)),
        ],
        out_shape=[
            jax.ShapeDtypeStruct((TOK, 2 * HW), F32),
            pltpu.HBM((2, 5, BLK, BLK), BF),
            pltpu.HBM((2, 5, BLK, BLK), BF),
        ],
        compiler_params=params(),
        cost_estimate=cost(3.2),
        name="near",
    )(keys, *streamed(turned), out_grad, weights, *after)


HALF = PART // 2


def begin_values_kernel(place, own, left, right, w_ref, *rest):
    me = place[1]
    total = None
    for distance, part in ((0, own), (3, left), (1, right)):
        at = pl.multiple_of(lax.rem(me + distance, 4) * PART, PART)
        term = dot(w_ref[:, pl.ds(at, PART)], part[...])
        total = term if total is None else total + term
    rest[-1][...] = total


def end_values_kernel(place, total_ref, fu, fl, w_upper, w_lower, k_ref, *rest):
    v_ref, state_ref = rest[-2:]
    tile = pl.program_id(0)
    core = place[0]
    far = dot(w_upper[...], fu[...]) + dot(w_lower[...], fl[...])
    v_ref[...] = (total_ref[...] + far).astype(BF)

    @pl.when(tile == 0)
    def _():
        state_ref[...] = jnp.zeros_like(state_ref)

    for slot in range(NH):
        at = pl.multiple_of(lax.rem(2 * (1 - core) + slot, NH) * HW, HW)
        state_ref[slot] += dot(v_ref[pl.ds(at, HW), :], k_ref[:, pl.ds(at, HW)])


def begin_values(place, parts, turned_weight, *after):
    wide = pl.BlockSpec((PART, BLK), lambda i, p: (0, i))
    return pl.pallas_call(
        begin_values_kernel,
        grid_spec=pltpu.PrefetchScalarGridSpec(
            num_scalar_prefetch=1,
            grid=(TOK // BLK,),
            in_specs=[wide] * 3 + [whole(NH * HW, 4 * PART)] + [ANY] * len(after),
            out_specs=wide,
        ),
        out_shape=jax.ShapeDtypeStruct((NH * HW, TOK), F32),
        compiler_params=params(),
        cost_estimate=cost(3.5),
        name="begin_values",
    )(place, *parts, turned_weight, *after)


def end_values(place, total, parts, turned_weight, keys, *after):
    tile = pl.BlockSpec((HALF, BLK), lambda i, p: (0, i))
    wide = pl.BlockSpec((PART, BLK), lambda i, p: (0, i))

    def weight(offset):
        return pl.BlockSpec((NH * HW, HALF), lambda i, p: (0, lax.rem(p[1] + 2, 4) * 2 + offset))

    return pl.pallas_call(
        end_values_kernel,
        grid_spec=pltpu.PrefetchScalarGridSpec(
            num_scalar_prefetch=1,
            grid=(TOK // BLK,),
            in_specs=[
                wide,
                tile,
                tile,
                weight(0),
                weight(1),
                pl.BlockSpec((BLK, NH * HW), lambda i, p: (i, 0)),
            ]
            + [ANY] * len(after),
            out_specs=[wide, pl.BlockSpec((NH, HW, HW), lambda i, p: (0, 0, 0))],
        ),
        out_shape=[
            pltpu.HBM((NH * HW, TOK), BF),
            jax.ShapeDtypeStruct((NH, HW, HW), F32),
        ],
        compiler_params=params(),
        cost_estimate=cost(3.7),
        name="end_values",
    )(place, total, *parts, turned_weight, turned_weight, keys, *after)


def share_out(place, term, plane, send_ref, keep_ref):
    core, col = place[0], place[2]
    for x in range(NX):
        turn = lax.rem(x - col + NX, NX)
        theirs = pl.multiple_of(x * 64 + (1 - core) * 32, 32)
        ours = pl.multiple_of(x * 64 + core * 32, 32)
        send_ref[turn, plane] = term[pl.ds(theirs, 32), :]
        keep_ref[turn, plane] = term[pl.ds(ours, 32), :]


def distance_of(step):
    return jnp.where(step == 0, 0, jnp.where(step == 1, 3, jnp.where(step == 2, 1, 2)))


def terms_kernel(place, near_a, near_b, k_ref, mine_ref, other_ref, *rest):
    own, left, right, fu, fl = rest[:5]
    send_ref, keep_ref, grad, term = rest[-4:]
    core = place[0]
    step = pl.program_id(0)

    @pl.when(step == 0)
    def _():
        for slot in range(NH):
            at = pl.multiple_of(lax.rem(2 * core + slot, NH) * HW, HW)
            state = mine_ref[slot] if slot < 2 else other_ref[slot - 2]
            far = dot(k_ref[:, pl.ds(at, HW)], state)
            columns = slice(slot % 2 * HW, (slot % 2 + 1) * HW)
            lower_heads = (core == 0) == (slot < 2)
            near = jnp.where(lower_heads, near_a[:, columns], near_b[:, columns])
            grad[:, pl.ds(at, HW)] = (near + far).astype(BF)

    halves = [(part.at[:HALF, :], part.at[HALF:, :]) for part in (own, left, right)]
    for index, pair in enumerate((*halves, (fu, fl))):

        @pl.when(step == index)
        def _(pair=pair):
            for plane in range(2):
                term[plane] = dot(pair[plane][...], grad[...])
                share_out(place, term.at[plane], plane, send_ref, keep_ref)


def shares():
    return pl.BlockSpec(
        (NX, 2, 32, NH * HW), lambda i, p: (0, lax.rem(p[1] + distance_of(i), 4), 0, 0)
    )


def weight_terms(place, near, keys, mine, other, parts, *after):
    return pl.pallas_call(
        terms_kernel,
        grid_spec=pltpu.PrefetchScalarGridSpec(
            num_scalar_prefetch=1,
            grid=(4,),
            in_specs=[
                whole(TOK, 2 * HW),
                whole(TOK, 2 * HW),
                whole(TOK, NH * HW),
                whole(2, HW, HW),
                whole(2, HW, HW),
            ]
            + [whole(PART, TOK)] * 3
            + [whole(HALF, TOK)] * 2
            + [ANY] * len(after),
            out_specs=[shares(), shares()],
            scratch_shapes=[
                pltpu.VMEM((TOK, NH * HW), BF),
                pltpu.VMEM((2, HALF, NH * HW), F32),
            ],
        ),
        out_shape=[
            jax.ShapeDtypeStruct((NX, NZ, 32, NH * HW), F32),
            pltpu.HBM((NX, NZ, 32, NH * HW), F32),
        ],
        compiler_params=params(),
        cost_estimate=cost(5),
        name="weight_terms",
    )(place, *near, keys, mine, other, *parts, *after)


def pair_kernel(place, kept_u, kept_l, got, own_ref, *messages):
    for plane, kept in enumerate((kept_u, kept_l)):
        own_ref[plane] = kept[0, 0] + got[0, plane]
        for turn in range(1, NX):
            messages[turn - 1][plane] = (kept[turn, 0] + got[turn, plane]).astype(BF)


def pair_sums(place, kept, got):
    def plane(offset):
        return pl.BlockSpec(
            (NX, 1, 32, NH * HW),
            lambda i, p: (0, 2 * lax.rem(p[1] + distance_of(i), 4) + offset, 0, 0),
        )

    return pl.pallas_call(
        pair_kernel,
        grid_spec=pltpu.PrefetchScalarGridSpec(
            num_scalar_prefetch=1,
            grid=(4,),
            in_specs=[plane(0), plane(1), shares()],
            out_specs=[
                pl.BlockSpec((2, 32, NH * HW), lambda i, p: (lax.rem(p[1] + distance_of(i), 4), 0, 0))
            ]
            * 4,
        ),
        out_shape=[jax.ShapeDtypeStruct((NZ, 32, NH * HW), F32)]
        + [jax.ShapeDtypeStruct((NZ, 32, NH * HW), BF)] * 3,
        compiler_params=params(),
        cost_estimate=cost(1.1),
        name="pair_sums",
    )(place, *streamed(kept, kept), got)


def far_product(levels, first, turned_ref, lw_ref, place, total, stack):
    head = lax.rem(2 * place[0] + pl.program_id(0), NH)
    rows = rows_of(lw_ref, DEPTH + 1 + first, 3, head)
    for index, level in enumerate(levels):
        stack[index * HW : (index + 1) * HW, :] = level
    product = dot(stack[...], turned_ref[0])
    for index in range(3):
        total = total + product[index * HW : (index + 1) * HW, :] * rows[index]
    return total


def begin_attended_kernel(place, turned_ref, lw_ref, v_ref, *rest):
    near_a, near_b, zero_ref, far_ref = rest[:2], rest[2:4], rest[4], rest[5]
    out_ref, stack = rest[-2:]
    lower_heads = (place[0] == 0) == (pl.program_id(0) < 2)

    def add(near_refs):
        for high in range(SIDES):
            columns = slice(high * BLK, (high + 1) * BLK)
            total = None
            for index, (low, other) in enumerate(SQUARES):
                if other == high:
                    term = dot(v_ref[:, low * BLK : (low + 1) * BLK], near_refs[index // 5][0, index % 5])
                    total = term if total is None else total + term
            out_ref[0, :, columns] = total

    pl.when(lower_heads)(lambda: add(near_a))
    pl.when(jnp.logical_not(lower_heads))(lambda: add(near_b))
    levels = (zero_ref[0], far_ref[0, 0], far_ref[1, 0])
    out_ref[0] = far_product(levels, 0, turned_ref, lw_ref, place, out_ref[0], stack)


def end_attended_kernel(place, turned_ref, lw_ref, total_u, total_l, far_ref, out_ref, stack):
    levels = (far_ref[0, 0], far_ref[1, 0], far_ref[2, 0])
    total = jnp.concatenate([total_u[0], total_l[0]], axis=0)
    total = far_product(levels, 3, turned_ref, lw_ref, place, total, stack)
    out_ref[...] = total.astype(BF).T


def begin_attended(place, turned, weights, values, near, zero, far, *after):
    def head(s, p):
        return lax.rem(2 * p[0] + s, NH)

    def pair(lower):
        def block(s, p):
            reads = (p[0] == 0) == (s < 2) if lower else (p[0] == 0) != (s < 2)
            idle = jnp.where(s < 2, 0, 1)
            return (jnp.where(reads, lax.rem(s, 2), idle), 0, 0, 0)

        return pl.BlockSpec((1, 5, BLK, BLK), block)

    return pl.pallas_call(
        begin_attended_kernel,
        grid_spec=pltpu.PrefetchScalarGridSpec(
            num_scalar_prefetch=1,
            grid=(NH,),
            in_specs=[
                pl.BlockSpec((1, HW, TOK), lambda s, p: (head(s, p), 0, 0)),
                LEVELS,
                pl.BlockSpec((HW, TOK), lambda s, p: (head(s, p), 0)),
                pair(True),
                pair(True),
                pair(False),
                pair(False),
                pl.BlockSpec((1, HW, HW), lambda s, p: (s, 0, 0)),
                pl.BlockSpec((2, 1, HW, HW), lambda s, p: (0, s, 0, 0)),
            ]
            + [ANY] * len(after),
            out_specs=pl.BlockSpec((1, HW, TOK), lambda s, p: (s, 0, 0)),
            scratch_shapes=[pltpu.VMEM((3 * HW, HW), BF)],
        ),
        out_shape=pltpu.HBM((NH, HW, TOK), F32),
        compiler_params=params(),
        cost_estimate=cost(0.3),
        name="begin_attended",
    )(
        place,
        *streamed(turned),
        weights,
        *streamed(values, *near),
        zero,
        far,
        *after,
    )


def end_attended(place, turned, weights, total, far):
    def head(s, p):
        return lax.rem(2 * p[0] + s, NH)

    return pl.pallas_call(
        end_attended_kernel,
        grid_spec=pltpu.PrefetchScalarGridSpec(
            num_scalar_prefetch=1,
            grid=(NH,),
            in_specs=[
                pl.BlockSpec((1, HW, TOK), lambda s, p: (head(s, p), 0, 0)),
                LEVELS,
                pl.BlockSpec((1, HW // 2, TOK), lambda s, p: (s, 0, 0)),
                pl.BlockSpec((1, HW // 2, TOK), lambda s, p: (s, 1, 0)),
                pl.BlockSpec((3, 1, HW, HW), lambda s, p: (0, s, 0, 0)),
            ],
            out_specs=pl.BlockSpec((TOK, HW), lambda s, p: (0, head(s, p))),
            scratch_shapes=[pltpu.VMEM((3 * HW, HW), BF)],
        ),
        out_shape=jax.ShapeDtypeStruct((TOK, NH * HW), BF),
        compiler_params=params(),
        cost_estimate=cost(0.3),
        name="end_attended",
    )(place, *streamed(turned), weights, *streamed(total, total), far)


def behind(value, *made):
    return lax.optimization_barrier((value, *made))[0]


def both(mine):
    return jnp.concatenate([mine, swap(mine, "core", 1, 2)], axis=1)


def local(hidden_in, value_weight, queries, keys, level_weights, out_grad):
    z, x, core, me = (lax.axis_index(a) for a in ("z", "x", "core", "head"))
    place = jnp.stack([core, me, x]).astype(jnp.int32)

    first, send, keep, turned_queries = query_states(place, queries, out_grad, level_weights)
    send_got = swap(send, "core", 1, 2)

    pairs = keep + send_got
    message = pairs[2:].astype(BF)

    (own,) = turned(hidden_in, BLK, 1, "turn_features", message)
    left = shift(own, "head", 1, 4)
    right = shift(own, "head", 3, 4)
    fu = shift(left[:HALF], "head", 1, 4)
    fl = shift(right[HALF:], "head", 3, 4)

    got = swap(message, "z", 1, NZ)
    total = jnp.where(z & 1 == 0, got[0].astype(F32), 0.0)
    level_4, level_5 = pairs[3] + got[1].astype(F32), pairs[4] + got[2].astype(F32)
    message = behind(jnp.stack([level_4, level_5]).astype(BF), own)
    got = swap(message, "z", 2, NZ)
    first_got = lax.ppermute(first, "core", [(1, 0)])
    back_a, *near_a = near(0, keys, turned_queries, out_grad, level_weights, message)
    (turned_weight,) = turned(value_weight, PART, 1, "turn_weight", message)
    total = total + jnp.where(z & 2 == 0, got[0].astype(F32), 0.0)
    message = behind((level_5 + got[1].astype(F32)).astype(BF), back_a, turned_weight)
    got = lax.ppermute(message, "z", [(i + 4, i) for i in range(4)])
    back_b, *near_b = near(2, keys, turned_queries, out_grad, level_weights, message)
    total = total + behind(got, back_b, left, right).astype(F32)
    summed = total
    for distance in (1, 3, 2):
        to = (x + distance) % NX
        level = jnp.where(to ^ x == 1, pairs[0], pairs[1])
        message = (total + jnp.where(to < x, level, 0.0)).astype(BF)
        summed = summed + shift(message, "x", distance, NX).astype(F32)
    begun = begin_values(place, (own, left, right), turned_weight, message)
    values, state = end_values(place, begun, (fu, fl), turned_weight, keys, message)
    other = swap(behind(summed, state), "core", 1, 2)
    mine = (summed + first_got[:2]).astype(BF)
    other = (other + first_got[2:]).astype(BF)

    got = swap(state, "core", 1, 2)
    zero = jnp.where(core == 1, got, 0.0).astype(BF)
    pair = state[2:] + got[:2]
    message = pair.astype(BF)
    parts = (own, left, right, fu, fl)
    send, keep = weight_terms(place, (back_a, back_b), keys, mine, other, parts, message)
    send_got = swap(send, "core", 1, 2)

    by_one, by_two, by_three = (shift(message, "x", d, NX).astype(F32) for d in (1, 2, 3))
    level_1 = jnp.where(x & 1 == 1, by_one, 0.0)
    level_2 = jnp.where(x == 2, by_one + by_two, jnp.where(x == 3, by_two + by_three, 0.0))
    running = pair + by_one + by_two + by_three
    rows, *messages = pair_sums(place, keep, send_got)
    message = behind(running.astype(BF), rows)
    first, second, third = (shift(messages[d - 1], "x", d, NX) for d in (1, 3, 2))
    rows = rows + first.astype(F32) + second.astype(F32) + third.astype(F32)
    got = swap(message, "z", 1, NZ).astype(F32)
    level_3 = jnp.where(z & 1 == 1, got, 0.0)
    running = running + got
    lower_levels = both(jnp.stack([level_1, level_2]).astype(BF))
    message = behind(running.astype(BF), first)
    got = swap(message, "z", 2, NZ).astype(F32)
    begun = begin_attended(
        place, turned_queries, level_weights, values, (*near_a, *near_b), zero, lower_levels, message
    )
    level_4 = jnp.where(z & 2 == 2, got, 0.0)
    running = running + got
    rows = rows.astype(BF)
    message = behind(running.astype(BF), begun)
    level_5 = lax.ppermute(message, "z", [(i, i + 4) for i in range(4)])
    rows = lax.all_to_all(rows, "z", 0, 0, tiled=True)
    weight_grad = rows.astype(F32).sum(axis=0)
    upper_levels = behind(jnp.stack([level_3.astype(BF), level_4.astype(BF), level_5]), rows)
    attended = end_attended(place, turned_queries, level_weights, begun, both(upper_levels))
    return attended, weight_grad


def solution(mesh):
    fine = Mesh(mesh.devices.reshape(NZ, NX, 2, 4), ("z", "x", "core", "head"))
    seq = ("z", "x", "core")
    return jax.shard_map(
        local,
        mesh=fine,
        in_specs=(
            P(seq, "head"),
            P(None, "head"),
            P(seq, "head"),
            P(seq, "head"),
            P(None, "head", seq),
            P(seq, "head"),
        ),
        out_specs=(P(seq, "head"), P(seq, "head")),
        check_vma=False,
    )
```

```python
import functools

import jax
import jax.numpy as jnp
from jax import lax
from jax.experimental import pallas as pl
from jax.experimental.pallas import tpu as pltpu
from jax.sharding import Mesh, PartitionSpec as P

BF = jnp.bfloat16
F32 = jnp.float32
HW = 128
NH = 4
TOK = 1024
BLK = 256
DEPTH = 10
FAR = 6
PART = 512
NX, NZ = 4, 8
VMEM = 24 * 1024 * 1024

NT = (((1,), (1,)), ((), ()))
TN = (((0,), (0,)), ((), ()))
NN = (((1,), (0,)), ((), ()))


def dot(a, b, dims=NN):
    return lax.dot_general(a, b, dims, preferred_element_type=F32)


def shift(value, axis, distance, size):
    return lax.ppermute(value, axis, [(i, (i + distance) % size) for i in range(size)])


def swap(value, axis, distance, size):
    return lax.ppermute(value, axis, [(i, i ^ distance) for i in range(size)])


def rows_of(lw_ref, first, count, head):
    rows = []
    for level in range(first, first + count):
        every = lw_ref[level].astype(F32)
        index = lax.broadcasted_iota(jnp.int32, every.shape, 0)
        rows.append(jnp.sum(jnp.where(index == head, every, 0.0), axis=0, keepdims=True))
    return rows


def whole(*shape):
    return pl.BlockSpec(shape, lambda *_: (0,) * len(shape))


LEVELS = whole(DEPTH + 1 + FAR, NH, TOK)


def params():
    return pltpu.CompilerParams(
        dimension_semantics=("arbitrary",), vmem_limit_bytes=VMEM
    )


def cost(us):
    return pl.CostEstimate(flops=int(us * 1.15e9), bytes_accessed=1000, transcendentals=0)


ANY = pl.BlockSpec(memory_space=pl.ANY)


def streamed(*values):
    return [pltpu.with_memory_space_constraint(value, pltpu.HBM) for value in values]


def turn_kernel(in_ref, *rest):
    turned = in_ref[...].T
    at = 0
    for out_ref in rest[1:]:
        out_ref[...] = turned[at : at + out_ref.shape[0], :]
        at += out_ref.shape[0]


def turned(value, side, count, name, after):
    rows, columns = value.shape
    part = columns // count
    return pl.pallas_call(
        turn_kernel,
        grid=(rows // side,),
        in_specs=[pl.BlockSpec((side, columns), lambda i: (i, 0)), ANY],
        out_specs=[pl.BlockSpec((part, side), lambda i: (0, i))] * count,
        out_shape=[jax.ShapeDtypeStruct((part, rows), value.dtype)] * count,
        compiler_params=params(),
        cost_estimate=cost(1.5),
        name=name,
    )(value, after)


def query_state_kernel(place, q_u, q_l, g_u, g_l, lw_ref, *rest):
    first_ref, send_ref, keep_ref, turned_ref, stack = rest[-5:]
    slot = pl.program_id(0)
    half = TOK // 2
    turned_ref[0, :, :half] = q_u[...].T
    turned_ref[0, :, half:] = q_l[...].T
    turned = turned_ref[0]
    head = lax.rem(2 * (1 - place[0]) + slot, NH)
    for digit, row in enumerate(rows_of(lw_ref, DEPTH + 1, FAR, head)):
        stack[digit * HW : (digit + 1) * HW, :] = turned * row.astype(BF)
    state = dot(stack[:, :half], g_u[...]) + dot(stack[:, half:], g_l[...])
    first_ref[0] = state[:HW]
    rest = state[HW:].reshape(FAR - 1, HW, HW)

    @pl.when(slot < 2)
    def _():
        send_ref[:, 0] = rest

    @pl.when(slot >= 2)
    def _():
        keep_ref[:, 0] = rest


def query_states(place, queries, out_grad, weights, *after):
    def head(s, place):
        return lax.rem(2 * (1 - place[0]) + s, NH)

    return pl.pallas_call(
        query_state_kernel,
        grid_spec=pltpu.PrefetchScalarGridSpec(
            num_scalar_prefetch=1,
            grid=(NH,),
            in_specs=[
                pl.BlockSpec((TOK // 2, HW), lambda s, p: (0, head(s, p))),
                pl.BlockSpec((TOK // 2, HW), lambda s, p: (1, head(s, p))),
                pl.BlockSpec((TOK // 2, HW), lambda s, p: (0, head(s, p))),
                pl.BlockSpec((TOK // 2, HW), lambda s, p: (1, head(s, p))),
                LEVELS,
            ]
            + [ANY] * len(after),
            out_specs=[
                pl.BlockSpec((1, HW, HW), lambda s, p: (s, 0, 0)),
                pl.BlockSpec((FAR - 1, 1, HW, HW), lambda s, p: (0, jnp.minimum(s, 1), 0, 0)),
                pl.BlockSpec((FAR - 1, 1, HW, HW), lambda s, p: (0, jnp.maximum(s - 2, 0), 0, 0)),
                pl.BlockSpec((1, HW, TOK), lambda s, p: (head(s, p), 0, 0)),
            ],
            scratch_shapes=[pltpu.VMEM((FAR * HW, TOK), BF)],
        ),
        out_shape=[
            jax.ShapeDtypeStruct((NH, HW, HW), F32),
            jax.ShapeDtypeStruct((FAR - 1, 2, HW, HW), F32),
            jax.ShapeDtypeStruct((FAR - 1, 2, HW, HW), F32),
            pltpu.HBM((NH, HW, TOK), BF),
        ],
        compiler_params=params(),
        cost_estimate=cost(4),
        name="query_states",
    )(place, *streamed(queries, queries, out_grad, out_grad, weights), *after)


SIDES = TOK // BLK
SQUARES = [(low, high) for low in range(SIDES) for high in range(low, SIDES)]


def diagonal(levels, start, differ, causal):
    columns = slice(start, start + HW)
    weight = jnp.broadcast_to(levels[0][:, columns], (HW, HW))
    for level in range(1, HW.bit_length()):
        weight = jnp.where(differ >= 1 << (level - 1), levels[level][:, columns], weight)
    return jnp.where(causal, weight, 0.0)


def near_kernel(base, k_ref, turned_ref, g_ref, lw_ref, *rest):
    back_ref, *near_refs = rest[-3:]
    levels = rows_of(lw_ref, 0, DEPTH + 1, base + pl.program_id(0))
    earlier = lax.broadcasted_iota(jnp.int32, (HW, HW), 0)
    later = lax.broadcasted_iota(jnp.int32, (HW, HW), 1)
    differ, causal = earlier ^ later, earlier <= later
    zero = jnp.zeros((HW, HW), BF)
    middle = HW.bit_length()
    total = None
    for index, (low, high) in enumerate(SQUARES):
        columns = slice(high * BLK, (high + 1) * BLK)
        scores = dot(k_ref[low * BLK : (low + 1) * BLK, :], turned_ref[0, :, columns])
        if low != high:
            level = BLK.bit_length() + (high ^ low).bit_length() - 1
            square = (scores * levels[level][:, columns]).astype(BF)
        else:
            start = high * BLK
            across = levels[middle][:, start + HW : start + BLK]
            upper = scores[:HW, :HW] * diagonal(levels, start, differ, causal)
            lower = scores[HW:, HW:] * diagonal(levels, start + HW, differ, causal)
            top = jnp.concatenate([upper, scores[:HW, HW:] * across], axis=1).astype(BF)
            square = jnp.concatenate(
                [top, jnp.concatenate([zero, lower.astype(BF)], axis=1)], axis=0
            )
        near_refs[index // 5][0, index % 5] = square
        term = dot(square, g_ref[columns, :])
        total = term if low == high else total + term
        if high == SIDES - 1:
            back_ref[low * BLK : (low + 1) * BLK, :] = total


def near(base, keys, turned, out_grad, weights, *after):
    head = pl.BlockSpec((TOK, HW), lambda h: (0, base + h))
    return pl.pallas_call(
        functools.partial(near_kernel, base),
        grid=(2,),
        in_specs=[head, pl.BlockSpec((1, HW, TOK), lambda h: (base + h, 0, 0)), head, LEVELS]
        + [ANY] * len(after),
        out_specs=[
            pl.BlockSpec((TOK, HW), lambda h: (0, h)),
            pl.BlockSpec((1, 5, BLK, BLK), lambda h: (h, 0, 0, 0)),
            pl.BlockSpec((1, 5, BLK, BLK), lambda h: (h, 0, 0, 0)),
        ],
        out_shape=[
            jax.ShapeDtypeStruct((TOK, 2 * HW), F32),
            pltpu.HBM((2, 5, BLK, BLK), BF),
            pltpu.HBM((2, 5, BLK, BLK), BF),
        ],
        compiler_params=params(),
        cost_estimate=cost(3.2),
        name="near",
    )(keys, *streamed(turned), out_grad, weights, *after)


HALF = PART // 2


def begin_values_kernel(place, own, left, right, w_ref, *rest):
    me = place[1]
    total = None
    for distance, part in ((0, own), (3, left), (1, right)):
        at = pl.multiple_of(lax.rem(me + distance, 4) * PART, PART)
        term = dot(w_ref[:, pl.ds(at, PART)], part[...])
        total = term if total is None else total + term
    rest[-1][...] = total


def end_values_kernel(place, total_ref, fu, fl, w_upper, w_lower, k_ref, *rest):
    v_ref, state_ref = rest[-2:]
    tile = pl.program_id(0)
    core = place[0]
    far = dot(w_upper[...], fu[...]) + dot(w_lower[...], fl[...])
    v_ref[...] = (total_ref[...] + far).astype(BF)

    @pl.when(tile == 0)
    def _():
        state_ref[...] = jnp.zeros_like(state_ref)

    for slot in range(NH):
        at = pl.multiple_of(lax.rem(2 * (1 - core) + slot, NH) * HW, HW)
        state_ref[slot] += dot(v_ref[pl.ds(at, HW), :], k_ref[:, pl.ds(at, HW)])


def begin_values(place, parts, turned_weight, *after):
    wide = pl.BlockSpec((PART, BLK), lambda i, p: (0, i))
    return pl.pallas_call(
        begin_values_kernel,
        grid_spec=pltpu.PrefetchScalarGridSpec(
            num_scalar_prefetch=1,
            grid=(TOK // BLK,),
            in_specs=[wide] * 3 + [whole(NH * HW, 4 * PART)] + [ANY] * len(after),
            out_specs=wide,
        ),
        out_shape=jax.ShapeDtypeStruct((NH * HW, TOK), F32),
        compiler_params=params(),
        cost_estimate=cost(3.5),
        name="begin_values",
    )(place, *parts, turned_weight, *after)


def end_values(place, total, parts, turned_weight, keys, *after):
    tile = pl.BlockSpec((HALF, BLK), lambda i, p: (0, i))
    wide = pl.BlockSpec((PART, BLK), lambda i, p: (0, i))

    def weight(offset):
        return pl.BlockSpec((NH * HW, HALF), lambda i, p: (0, lax.rem(p[1] + 2, 4) * 2 + offset))

    return pl.pallas_call(
        end_values_kernel,
        grid_spec=pltpu.PrefetchScalarGridSpec(
            num_scalar_prefetch=1,
            grid=(TOK // BLK,),
            in_specs=[
                wide,
                tile,
                tile,
                weight(0),
                weight(1),
                pl.BlockSpec((BLK, NH * HW), lambda i, p: (i, 0)),
            ]
            + [ANY] * len(after),
            out_specs=[wide, pl.BlockSpec((NH, HW, HW), lambda i, p: (0, 0, 0))],
        ),
        out_shape=[
            pltpu.HBM((NH * HW, TOK), BF),
            jax.ShapeDtypeStruct((NH, HW, HW), F32),
        ],
        compiler_params=params(),
        cost_estimate=cost(3.7),
        name="end_values",
    )(place, total, *parts, turned_weight, turned_weight, keys, *after)


def share_out(place, term, plane, send_ref, keep_ref):
    core, col = place[0], place[2]
    for x in range(NX):
        turn = lax.rem(x - col + NX, NX)
        theirs = pl.multiple_of(x * 64 + (1 - core) * 32, 32)
        ours = pl.multiple_of(x * 64 + core * 32, 32)
        send_ref[turn, plane] = term[pl.ds(theirs, 32), :]
        keep_ref[turn, plane] = term[pl.ds(ours, 32), :]


def distance_of(step):
    return jnp.where(step == 0, 0, jnp.where(step == 1, 3, jnp.where(step == 2, 1, 2)))


def terms_kernel(place, near_a, near_b, k_ref, mine_ref, other_ref, *rest):
    own, left, right, fu, fl = rest[:5]
    send_ref, keep_ref, grad, term = rest[-4:]
    core = place[0]
    step = pl.program_id(0)

    @pl.when(step == 0)
    def _():
        for slot in range(NH):
            at = pl.multiple_of(lax.rem(2 * core + slot, NH) * HW, HW)
            state = mine_ref[slot] if slot < 2 else other_ref[slot - 2]
            far = dot(k_ref[:, pl.ds(at, HW)], state)
            columns = slice(slot % 2 * HW, (slot % 2 + 1) * HW)
            lower_heads = (core == 0) == (slot < 2)
            near = jnp.where(lower_heads, near_a[:, columns], near_b[:, columns])
            grad[:, pl.ds(at, HW)] = (near + far).astype(BF)

    halves = [(part.at[:HALF, :], part.at[HALF:, :]) for part in (own, left, right)]
    for index, pair in enumerate((*halves, (fu, fl))):

        @pl.when(step == index)
        def _(pair=pair):
            for plane in range(2):
                term[plane] = dot(pair[plane][...], grad[...])
                share_out(place, term.at[plane], plane, send_ref, keep_ref)


def shares():
    return pl.BlockSpec(
        (NX, 2, 32, NH * HW), lambda i, p: (0, lax.rem(p[1] + distance_of(i), 4), 0, 0)
    )


def weight_terms(place, near, keys, mine, other, parts, *after):
    return pl.pallas_call(
        terms_kernel,
        grid_spec=pltpu.PrefetchScalarGridSpec(
            num_scalar_prefetch=1,
            grid=(4,),
            in_specs=[
                whole(TOK, 2 * HW),
                whole(TOK, 2 * HW),
                whole(TOK, NH * HW),
                whole(2, HW, HW),
                whole(2, HW, HW),
            ]
            + [whole(PART, TOK)] * 3
            + [whole(HALF, TOK)] * 2
            + [ANY] * len(after),
            out_specs=[shares(), shares()],
            scratch_shapes=[
                pltpu.VMEM((TOK, NH * HW), BF),
                pltpu.VMEM((2, HALF, NH * HW), F32),
            ],
        ),
        out_shape=[
            jax.ShapeDtypeStruct((NX, NZ, 32, NH * HW), F32),
            pltpu.HBM((NX, NZ, 32, NH * HW), F32),
        ],
        compiler_params=params(),
        cost_estimate=cost(5),
        name="weight_terms",
    )(place, *near, keys, mine, other, *parts, *after)


def pair_kernel(place, kept_u, kept_l, got, own_ref, *messages):
    for plane, kept in enumerate((kept_u, kept_l)):
        own_ref[plane] = kept[0, 0] + got[0, plane]
        for turn in range(1, NX):
            messages[turn - 1][plane] = (kept[turn, 0] + got[turn, plane]).astype(BF)


def pair_sums(place, kept, got):
    def plane(offset):
        return pl.BlockSpec(
            (NX, 1, 32, NH * HW),
            lambda i, p: (0, 2 * lax.rem(p[1] + distance_of(i), 4) + offset, 0, 0),
        )

    return pl.pallas_call(
        pair_kernel,
        grid_spec=pltpu.PrefetchScalarGridSpec(
            num_scalar_prefetch=1,
            grid=(4,),
            in_specs=[plane(0), plane(1), shares()],
            out_specs=[
                pl.BlockSpec((2, 32, NH * HW), lambda i, p: (lax.rem(p[1] + distance_of(i), 4), 0, 0))
            ]
            * 4,
        ),
        out_shape=[jax.ShapeDtypeStruct((NZ, 32, NH * HW), F32)]
        + [jax.ShapeDtypeStruct((NZ, 32, NH * HW), BF)] * 3,
        compiler_params=params(),
        cost_estimate=cost(1.1),
        name="pair_sums",
    )(place, *streamed(kept, kept), got)


def far_product(levels, first, turned_ref, lw_ref, place, total, stack):
    head = lax.rem(2 * place[0] + pl.program_id(0), NH)
    rows = rows_of(lw_ref, DEPTH + 1 + first, 3, head)
    for index, level in enumerate(levels):
        stack[index * HW : (index + 1) * HW, :] = level
    product = dot(stack[...], turned_ref[0])
    for index in range(3):
        total = total + product[index * HW : (index + 1) * HW, :] * rows[index]
    return total


def begin_attended_kernel(place, turned_ref, lw_ref, v_ref, *rest):
    near_a, near_b, zero_ref, far_ref = rest[:2], rest[2:4], rest[4], rest[5]
    out_ref, stack = rest[-2:]
    lower_heads = (place[0] == 0) == (pl.program_id(0) < 2)

    def add(near_refs):
        for high in range(SIDES):
            columns = slice(high * BLK, (high + 1) * BLK)
            total = None
            for index, (low, other) in enumerate(SQUARES):
                if other == high:
                    term = dot(v_ref[:, low * BLK : (low + 1) * BLK], near_refs[index // 5][0, index % 5])
                    total = term if total is None else total + term
            out_ref[0, :, columns] = total

    pl.when(lower_heads)(lambda: add(near_a))
    pl.when(jnp.logical_not(lower_heads))(lambda: add(near_b))
    levels = (zero_ref[0], far_ref[0, 0], far_ref[1, 0])
    out_ref[0] = far_product(levels, 0, turned_ref, lw_ref, place, out_ref[0], stack)


def end_attended_kernel(place, turned_ref, lw_ref, total_u, total_l, far_ref, out_ref, stack):
    levels = (far_ref[0, 0], far_ref[1, 0], far_ref[2, 0])
    total = jnp.concatenate([total_u[0], total_l[0]], axis=0)
    total = far_product(levels, 3, turned_ref, lw_ref, place, total, stack)
    out_ref[...] = total.astype(BF).T


def begin_attended(place, turned, weights, values, near, zero, far, *after):
    def head(s, p):
        return lax.rem(2 * p[0] + s, NH)

    def pair(lower):
        def block(s, p):
            reads = (p[0] == 0) == (s < 2) if lower else (p[0] == 0) != (s < 2)
            idle = jnp.where(s < 2, 0, 1)
            return (jnp.where(reads, lax.rem(s, 2), idle), 0, 0, 0)

        return pl.BlockSpec((1, 5, BLK, BLK), block)

    return pl.pallas_call(
        begin_attended_kernel,
        grid_spec=pltpu.PrefetchScalarGridSpec(
            num_scalar_prefetch=1,
            grid=(NH,),
            in_specs=[
                pl.BlockSpec((1, HW, TOK), lambda s, p: (head(s, p), 0, 0)),
                LEVELS,
                pl.BlockSpec((HW, TOK), lambda s, p: (head(s, p), 0)),
                pair(True),
                pair(True),
                pair(False),
                pair(False),
                pl.BlockSpec((1, HW, HW), lambda s, p: (s, 0, 0)),
                pl.BlockSpec((2, 1, HW, HW), lambda s, p: (0, s, 0, 0)),
            ]
            + [ANY] * len(after),
            out_specs=pl.BlockSpec((1, HW, TOK), lambda s, p: (s, 0, 0)),
            scratch_shapes=[pltpu.VMEM((3 * HW, HW), BF)],
        ),
        out_shape=pltpu.HBM((NH, HW, TOK), F32),
        compiler_params=params(),
        cost_estimate=cost(0.3),
        name="begin_attended",
    )(
        place,
        *streamed(turned),
        weights,
        *streamed(values, *near),
        zero,
        far,
        *after,
    )


def end_attended(place, turned, weights, total, far):
    def head(s, p):
        return lax.rem(2 * p[0] + s, NH)

    return pl.pallas_call(
        end_attended_kernel,
        grid_spec=pltpu.PrefetchScalarGridSpec(
            num_scalar_prefetch=1,
            grid=(NH,),
            in_specs=[
                pl.BlockSpec((1, HW, TOK), lambda s, p: (head(s, p), 0, 0)),
                LEVELS,
                pl.BlockSpec((1, HW // 2, TOK), lambda s, p: (s, 0, 0)),
                pl.BlockSpec((1, HW // 2, TOK), lambda s, p: (s, 1, 0)),
                pl.BlockSpec((3, 1, HW, HW), lambda s, p: (0, s, 0, 0)),
            ],
            out_specs=pl.BlockSpec((TOK, HW), lambda s, p: (0, head(s, p))),
            scratch_shapes=[pltpu.VMEM((3 * HW, HW), BF)],
        ),
        out_shape=jax.ShapeDtypeStruct((TOK, NH * HW), BF),
        compiler_params=params(),
        cost_estimate=cost(0.3),
        name="end_attended",
    )(place, *streamed(turned), weights, *streamed(total, total), far)


def behind(value, *made):
    return lax.optimization_barrier((value, *made))[0]


def both(mine):
    return jnp.concatenate([mine, swap(mine, "core", 1, 2)], axis=1)


def local(hidden_in, value_weight, queries, keys, level_weights, out_grad):
    z, x, core, me = (lax.axis_index(a) for a in ("z", "x", "core", "head"))
    place = jnp.stack([core, me, x]).astype(jnp.int32)

    first, send, keep, turned_queries = query_states(place, queries, out_grad, level_weights)
    send_got = swap(send, "core", 1, 2)

    pairs = keep + send_got
    message = pairs[2:].astype(BF)

    (own,) = turned(hidden_in, BLK, 1, "turn_features", message)
    left = shift(own, "head", 1, 4)
    right = shift(own, "head", 3, 4)
    fu = shift(left[:HALF], "head", 1, 4)
    fl = shift(right[HALF:], "head", 3, 4)

    got = swap(message, "z", 1, NZ)
    total = jnp.where(z & 1 == 0, got[0].astype(F32), 0.0)
    level_4, level_5 = pairs[3] + got[1].astype(F32), pairs[4] + got[2].astype(F32)
    message = behind(jnp.stack([level_4, level_5]).astype(BF), own)
    got = swap(message, "z", 2, NZ)
    first_got = lax.ppermute(first, "core", [(1, 0)])
    back_a, *near_a = near(0, keys, turned_queries, out_grad, level_weights, message)
    (turned_weight,) = turned(value_weight, PART, 1, "turn_weight", message)
    total = total + jnp.where(z & 2 == 0, got[0].astype(F32), 0.0)
    message = behind((level_5 + got[1].astype(F32)).astype(BF), back_a, turned_weight)
    got = lax.ppermute(message, "z", [(i + 4, i) for i in range(4)])
    back_b, *near_b = near(2, keys, turned_queries, out_grad, level_weights, message)
    total = total + behind(got, back_b, left, right).astype(F32)
    summed = total
    for distance in (1, 3, 2):
        to = (x + distance) % NX
        level = jnp.where(to ^ x == 1, pairs[0], pairs[1])
        message = (total + jnp.where(to < x, level, 0.0)).astype(BF)
        summed = summed + shift(message, "x", distance, NX).astype(F32)
    begun = begin_values(place, (own, left, right), turned_weight, message)
    values, state = end_values(place, begun, (fu, fl), turned_weight, keys, message)
    other = swap(behind(summed, state), "core", 1, 2)
    mine = (summed + first_got[:2]).astype(BF)
    other = (other + first_got[2:]).astype(BF)

    got = swap(state, "core", 1, 2)
    zero = jnp.where(core == 1, got, 0.0).astype(BF)
    pair = state[2:] + got[:2]
    message = pair.astype(BF)
    parts = (own, left, right, fu, fl)
    send, keep = weight_terms(place, (back_a, back_b), keys, mine, other, parts, message)
    send_got = swap(send, "core", 1, 2)

    by_one, by_two, by_three = (shift(message, "x", d, NX).astype(F32) for d in (1, 2, 3))
    level_1 = jnp.where(x & 1 == 1, by_one, 0.0)
    level_2 = jnp.where(x == 2, by_one + by_two, jnp.where(x == 3, by_two + by_three, 0.0))
    running = pair + by_one + by_two + by_three
    rows, *messages = pair_sums(place, keep, send_got)
    message = behind(running.astype(BF), rows)
    first, second, third = (shift(messages[d - 1], "x", d, NX) for d in (1, 3, 2))
    rows = rows + first.astype(F32) + second.astype(F32) + third.astype(F32)
    lower_levels = both(jnp.stack([level_1, level_2]).astype(BF))
    begun = begin_attended(
        place, turned_queries, level_weights, values, (*near_a, *near_b), zero, lower_levels, message
    )
    got = swap(message, "z", 1, NZ).astype(F32)
    level_3 = jnp.where(z & 1 == 1, got, 0.0)
    running = running + got
    rows = rows.astype(BF)
    message = behind(running.astype(BF), begun, rows)
    got = swap(message, "z", 2, NZ).astype(F32)
    level_4 = jnp.where(z & 2 == 2, got, 0.0)
    running = running + got
    message = running.astype(BF)
    level_5 = lax.ppermute(message, "z", [(i, i + 4) for i in range(4)])
    rows = lax.all_to_all(rows, "z", 0, 0, tiled=True)
    weight_grad = rows.astype(F32).sum(axis=0)
    upper_levels = jnp.stack([level_3.astype(BF), level_4.astype(BF), level_5])
    attended = end_attended(place, turned_queries, level_weights, begun, both(upper_levels))
    return attended, weight_grad


def solution(mesh):
    fine = Mesh(mesh.devices.reshape(NZ, NX, 2, 4), ("z", "x", "core", "head"))
    seq = ("z", "x", "core")
    return jax.shard_map(
        local,
        mesh=fine,
        in_specs=(
            P(seq, "head"),
            P(None, "head"),
            P(seq, "head"),
            P(seq, "head"),
            P(None, "head", seq),
            P(seq, "head"),
        ),
        out_specs=(P(seq, "head"), P(seq, "head")),
        check_vma=False,
    )
```

```python
import functools

import jax
import jax.numpy as jnp
from jax import lax
from jax.experimental import pallas as pl
from jax.experimental.pallas import tpu as pltpu
from jax.sharding import Mesh, PartitionSpec as P

BF = jnp.bfloat16
F32 = jnp.float32
HW = 128
NH = 4
TOK = 1024
BLK = 256
DEPTH = 10
FAR = 6
PART = 512
NX, NZ = 4, 8
VMEM = 24 * 1024 * 1024

NT = (((1,), (1,)), ((), ()))
TN = (((0,), (0,)), ((), ()))
NN = (((1,), (0,)), ((), ()))


def dot(a, b, dims=NN):
    return lax.dot_general(a, b, dims, preferred_element_type=F32)


def shift(value, axis, distance, size):
    return lax.ppermute(value, axis, [(i, (i + distance) % size) for i in range(size)])


def swap(value, axis, distance, size):
    return lax.ppermute(value, axis, [(i, i ^ distance) for i in range(size)])


def rows_of(lw_ref, first, count, head):
    rows = []
    for level in range(first, first + count):
        every = lw_ref[level].astype(F32)
        index = lax.broadcasted_iota(jnp.int32, every.shape, 0)
        rows.append(jnp.sum(jnp.where(index == head, every, 0.0), axis=0, keepdims=True))
    return rows


def whole(*shape):
    return pl.BlockSpec(shape, lambda *_: (0,) * len(shape))


LEVELS = whole(DEPTH + 1 + FAR, NH, TOK)


def params():
    return pltpu.CompilerParams(
        dimension_semantics=("arbitrary",), vmem_limit_bytes=VMEM
    )


def cost(us):
    return pl.CostEstimate(flops=int(us * 1.15e9), bytes_accessed=1000, transcendentals=0)


ANY = pl.BlockSpec(memory_space=pl.ANY)


def streamed(*values):
    return [pltpu.with_memory_space_constraint(value, pltpu.HBM) for value in values]


def turn_kernel(in_ref, *rest):
    turned = in_ref[...].T
    at = 0
    for out_ref in rest[1:]:
        out_ref[...] = turned[at : at + out_ref.shape[0], :]
        at += out_ref.shape[0]


def turned(value, side, count, name, after):
    rows, columns = value.shape
    part = columns // count
    return pl.pallas_call(
        turn_kernel,
        grid=(rows // side,),
        in_specs=[pl.BlockSpec((side, columns), lambda i: (i, 0)), ANY],
        out_specs=[pl.BlockSpec((part, side), lambda i: (0, i))] * count,
        out_shape=[jax.ShapeDtypeStruct((part, rows), value.dtype)] * count,
        compiler_params=params(),
        cost_estimate=cost(1.5),
        name=name,
    )(value, after)


def query_state_kernel(place, q_u, q_l, g_u, g_l, lw_ref, *rest):
    first_ref, send_ref, keep_ref, turned_ref, stack = rest[-5:]
    slot = pl.program_id(0)
    half = TOK // 2
    turned_ref[0, :, :half] = q_u[...].T
    turned_ref[0, :, half:] = q_l[...].T
    turned = turned_ref[0]
    head = lax.rem(2 * (1 - place[0]) + slot, NH)
    for digit, row in enumerate(rows_of(lw_ref, DEPTH + 1, FAR, head)):
        stack[digit * HW : (digit + 1) * HW, :] = turned * row.astype(BF)
    state = dot(stack[:, :half], g_u[...]) + dot(stack[:, half:], g_l[...])
    first_ref[0] = state[:HW]
    rest = state[HW:].reshape(FAR - 1, HW, HW)

    @pl.when(slot < 2)
    def _():
        send_ref[:, 0] = rest

    @pl.when(slot >= 2)
    def _():
        keep_ref[:, 0] = rest


def query_states(place, queries, out_grad, weights, *after):
    def head(s, place):
        return lax.rem(2 * (1 - place[0]) + s, NH)

    return pl.pallas_call(
        query_state_kernel,
        grid_spec=pltpu.PrefetchScalarGridSpec(
            num_scalar_prefetch=1,
            grid=(NH,),
            in_specs=[
                pl.BlockSpec((TOK // 2, HW), lambda s, p: (0, head(s, p))),
                pl.BlockSpec((TOK // 2, HW), lambda s, p: (1, head(s, p))),
                pl.BlockSpec((TOK // 2, HW), lambda s, p: (0, head(s, p))),
                pl.BlockSpec((TOK // 2, HW), lambda s, p: (1, head(s, p))),
                LEVELS,
            ]
            + [ANY] * len(after),
            out_specs=[
                pl.BlockSpec((1, HW, HW), lambda s, p: (s, 0, 0)),
                pl.BlockSpec((FAR - 1, 1, HW, HW), lambda s, p: (0, jnp.minimum(s, 1), 0, 0)),
                pl.BlockSpec((FAR - 1, 1, HW, HW), lambda s, p: (0, jnp.maximum(s - 2, 0), 0, 0)),
                pl.BlockSpec((1, HW, TOK), lambda s, p: (head(s, p), 0, 0)),
            ],
            scratch_shapes=[pltpu.VMEM((FAR * HW, TOK), BF)],
        ),
        out_shape=[
            jax.ShapeDtypeStruct((NH, HW, HW), F32),
            jax.ShapeDtypeStruct((FAR - 1, 2, HW, HW), F32),
            jax.ShapeDtypeStruct((FAR - 1, 2, HW, HW), F32),
            pltpu.HBM((NH, HW, TOK), BF),
        ],
        compiler_params=params(),
        cost_estimate=cost(4),
        name="query_states",
    )(place, *streamed(queries, queries, out_grad, out_grad, weights), *after)


SIDES = TOK // BLK
SQUARES = [(low, high) for low in range(SIDES) for high in range(low, SIDES)]


def diagonal(levels, start, differ, causal):
    columns = slice(start, start + HW)
    weight = jnp.broadcast_to(levels[0][:, columns], (HW, HW))
    for level in range(1, HW.bit_length()):
        weight = jnp.where(differ >= 1 << (level - 1), levels[level][:, columns], weight)
    return jnp.where(causal, weight, 0.0)


def near_kernel(base, k_ref, turned_ref, g_ref, lw_ref, *rest):
    back_ref, *near_refs = rest[-3:]
    levels = rows_of(lw_ref, 0, DEPTH + 1, base + pl.program_id(0))
    earlier = lax.broadcasted_iota(jnp.int32, (HW, HW), 0)
    later = lax.broadcasted_iota(jnp.int32, (HW, HW), 1)
    differ, causal = earlier ^ later, earlier <= later
    zero = jnp.zeros((HW, HW), BF)
    middle = HW.bit_length()
    total = None
    for index, (low, high) in enumerate(SQUARES):
        columns = slice(high * BLK, (high + 1) * BLK)
        scores = dot(k_ref[low * BLK : (low + 1) * BLK, :], turned_ref[0, :, columns])
        if low != high:
            level = BLK.bit_length() + (high ^ low).bit_length() - 1
            square = (scores * levels[level][:, columns]).astype(BF)
        else:
            start = high * BLK
            across = levels[middle][:, start + HW : start + BLK]
            upper = scores[:HW, :HW] * diagonal(levels, start, differ, causal)
            lower = scores[HW:, HW:] * diagonal(levels, start + HW, differ, causal)
            top = jnp.concatenate([upper, scores[:HW, HW:] * across], axis=1).astype(BF)
            square = jnp.concatenate(
                [top, jnp.concatenate([zero, lower.astype(BF)], axis=1)], axis=0
            )
        near_refs[index // 5][0, index % 5] = square
        term = dot(square, g_ref[columns, :])
        total = term if low == high else total + term
        if high == SIDES - 1:
            back_ref[low * BLK : (low + 1) * BLK, :] = total


def near(base, keys, turned, out_grad, weights, *after):
    head = pl.BlockSpec((TOK, HW), lambda h: (0, base + h))
    return pl.pallas_call(
        functools.partial(near_kernel, base),
        grid=(2,),
        in_specs=[head, pl.BlockSpec((1, HW, TOK), lambda h: (base + h, 0, 0)), head, LEVELS]
        + [ANY] * len(after),
        out_specs=[
            pl.BlockSpec((TOK, HW), lambda h: (0, h)),
            pl.BlockSpec((1, 5, BLK, BLK), lambda h: (h, 0, 0, 0)),
            pl.BlockSpec((1, 5, BLK, BLK), lambda h: (h, 0, 0, 0)),
        ],
        out_shape=[
            jax.ShapeDtypeStruct((TOK, 2 * HW), F32),
            pltpu.HBM((2, 5, BLK, BLK), BF),
            pltpu.HBM((2, 5, BLK, BLK), BF),
        ],
        compiler_params=params(),
        cost_estimate=cost(3.2),
        name="near",
    )(keys, *streamed(turned), out_grad, weights, *after)


HALF = PART // 2


def begin_values_kernel(place, own, left, right, w_ref, *rest):
    me = place[1]
    total = None
    for distance, part in ((0, own), (3, left), (1, right)):
        at = pl.multiple_of(lax.rem(me + distance, 4) * PART, PART)
        term = dot(w_ref[:, pl.ds(at, PART)], part[...])
        total = term if total is None else total + term
    rest[-1][...] = total


def end_values_kernel(place, total_ref, fu, fl, w_upper, w_lower, k_ref, *rest):
    v_ref, state_ref = rest[-2:]
    tile = pl.program_id(0)
    core = place[0]
    far = dot(w_upper[...], fu[...]) + dot(w_lower[...], fl[...])
    v_ref[...] = (total_ref[...] + far).astype(BF)

    @pl.when(tile == 0)
    def _():
        state_ref[...] = jnp.zeros_like(state_ref)

    for slot in range(NH):
        at = pl.multiple_of(lax.rem(2 * (1 - core) + slot, NH) * HW, HW)
        state_ref[slot] += dot(v_ref[pl.ds(at, HW), :], k_ref[:, pl.ds(at, HW)])


def begin_values(place, parts, turned_weight, *after):
    wide = pl.BlockSpec((PART, BLK), lambda i, p: (0, i))
    return pl.pallas_call(
        begin_values_kernel,
        grid_spec=pltpu.PrefetchScalarGridSpec(
            num_scalar_prefetch=1,
            grid=(TOK // BLK,),
            in_specs=[wide] * 3 + [whole(NH * HW, 4 * PART)] + [ANY] * len(after),
            out_specs=wide,
        ),
        out_shape=jax.ShapeDtypeStruct((NH * HW, TOK), F32),
        compiler_params=params(),
        cost_estimate=cost(3.5),
        name="begin_values",
    )(place, *parts, turned_weight, *after)


def end_values(place, total, parts, turned_weight, keys, *after):
    tile = pl.BlockSpec((HALF, BLK), lambda i, p: (0, i))
    wide = pl.BlockSpec((PART, BLK), lambda i, p: (0, i))

    def weight(offset):
        return pl.BlockSpec((NH * HW, HALF), lambda i, p: (0, lax.rem(p[1] + 2, 4) * 2 + offset))

    return pl.pallas_call(
        end_values_kernel,
        grid_spec=pltpu.PrefetchScalarGridSpec(
            num_scalar_prefetch=1,
            grid=(TOK // BLK,),
            in_specs=[
                wide,
                tile,
                tile,
                weight(0),
                weight(1),
                pl.BlockSpec((BLK, NH * HW), lambda i, p: (i, 0)),
            ]
            + [ANY] * len(after),
            out_specs=[wide, pl.BlockSpec((NH, HW, HW), lambda i, p: (0, 0, 0))],
        ),
        out_shape=[
            pltpu.HBM((NH * HW, TOK), BF),
            jax.ShapeDtypeStruct((NH, HW, HW), F32),
        ],
        compiler_params=params(),
        cost_estimate=cost(3.7),
        name="end_values",
    )(place, total, *parts, turned_weight, turned_weight, keys, *after)


def share_out(place, term, plane, send_ref, keep_ref):
    core, col = place[0], place[2]
    for x in range(NX):
        turn = lax.rem(x - col + NX, NX)
        theirs = pl.multiple_of(x * 64 + (1 - core) * 32, 32)
        ours = pl.multiple_of(x * 64 + core * 32, 32)
        send_ref[turn, plane] = term[pl.ds(theirs, 32), :]
        keep_ref[turn, plane] = term[pl.ds(ours, 32), :]


def distance_of(step):
    return jnp.where(step == 0, 0, jnp.where(step == 1, 3, jnp.where(step == 2, 1, 2)))


def terms_kernel(place, near_a, near_b, k_ref, mine_ref, other_ref, *rest):
    own, left, right, fu, fl = rest[:5]
    send_ref, keep_ref, grad, term = rest[-4:]
    core = place[0]
    step = pl.program_id(0)

    @pl.when(step == 0)
    def _():
        for slot in range(NH):
            at = pl.multiple_of(lax.rem(2 * core + slot, NH) * HW, HW)
            state = mine_ref[slot] if slot < 2 else other_ref[slot - 2]
            far = dot(k_ref[:, pl.ds(at, HW)], state)
            columns = slice(slot % 2 * HW, (slot % 2 + 1) * HW)
            lower_heads = (core == 0) == (slot < 2)
            near = jnp.where(lower_heads, near_a[:, columns], near_b[:, columns])
            grad[:, pl.ds(at, HW)] = (near + far).astype(BF)

    halves = [(part.at[:HALF, :], part.at[HALF:, :]) for part in (own, left, right)]
    for index, pair in enumerate((*halves, (fu, fl))):

        @pl.when(step == index)
        def _(pair=pair):
            for plane in range(2):
                term[plane] = dot(pair[plane][...], grad[...])
                share_out(place, term.at[plane], plane, send_ref, keep_ref)


def shares():
    return pl.BlockSpec(
        (NX, 2, 32, NH * HW), lambda i, p: (0, lax.rem(p[1] + distance_of(i), 4), 0, 0)
    )


def weight_terms(place, near, keys, mine, other, parts, *after):
    return pl.pallas_call(
        terms_kernel,
        grid_spec=pltpu.PrefetchScalarGridSpec(
            num_scalar_prefetch=1,
            grid=(4,),
            in_specs=[
                whole(TOK, 2 * HW),
                whole(TOK, 2 * HW),
                whole(TOK, NH * HW),
                whole(2, HW, HW),
                whole(2, HW, HW),
            ]
            + [whole(PART, TOK)] * 3
            + [whole(HALF, TOK)] * 2
            + [ANY] * len(after),
            out_specs=[shares(), shares()],
            scratch_shapes=[
                pltpu.VMEM((TOK, NH * HW), BF),
                pltpu.VMEM((2, HALF, NH * HW), F32),
            ],
        ),
        out_shape=[
            jax.ShapeDtypeStruct((NX, NZ, 32, NH * HW), F32),
            pltpu.HBM((NX, NZ, 32, NH * HW), F32),
        ],
        compiler_params=params(),
        cost_estimate=cost(5),
        name="weight_terms",
    )(place, *near, keys, mine, other, *parts, *after)


def pair_kernel(place, kept_u, kept_l, got, own_ref, *messages):
    for plane, kept in enumerate((kept_u, kept_l)):
        own_ref[plane] = kept[0, 0] + got[0, plane]
        for turn in range(1, NX):
            messages[turn - 1][plane] = (kept[turn, 0] + got[turn, plane]).astype(BF)


def pair_sums(place, kept, got):
    def plane(offset):
        return pl.BlockSpec(
            (NX, 1, 32, NH * HW),
            lambda i, p: (0, 2 * lax.rem(p[1] + distance_of(i), 4) + offset, 0, 0),
        )

    return pl.pallas_call(
        pair_kernel,
        grid_spec=pltpu.PrefetchScalarGridSpec(
            num_scalar_prefetch=1,
            grid=(4,),
            in_specs=[plane(0), plane(1), shares()],
            out_specs=[
                pl.BlockSpec((2, 32, NH * HW), lambda i, p: (lax.rem(p[1] + distance_of(i), 4), 0, 0))
            ]
            * 4,
        ),
        out_shape=[jax.ShapeDtypeStruct((NZ, 32, NH * HW), F32)]
        + [jax.ShapeDtypeStruct((NZ, 32, NH * HW), BF)] * 3,
        compiler_params=params(),
        cost_estimate=cost(1.1),
        name="pair_sums",
    )(place, *streamed(kept, kept), got)


def far_product(levels, first, turned_ref, lw_ref, place, total, stack):
    head = lax.rem(2 * place[0] + pl.program_id(0), NH)
    rows = rows_of(lw_ref, DEPTH + 1 + first, 3, head)
    for index, level in enumerate(levels):
        stack[index * HW : (index + 1) * HW, :] = level
    product = dot(stack[...], turned_ref[0])
    for index in range(3):
        total = total + product[index * HW : (index + 1) * HW, :] * rows[index]
    return total


def begin_attended_kernel(place, turned_ref, lw_ref, v_ref, *rest):
    near_a, near_b, zero_ref, far_ref = rest[:2], rest[2:4], rest[4], rest[5]
    out_ref, stack = rest[-2:]
    lower_heads = (place[0] == 0) == (pl.program_id(0) < 2)

    def add(near_refs):
        for high in range(SIDES):
            columns = slice(high * BLK, (high + 1) * BLK)
            total = None
            for index, (low, other) in enumerate(SQUARES):
                if other == high:
                    term = dot(v_ref[:, low * BLK : (low + 1) * BLK], near_refs[index // 5][0, index % 5])
                    total = term if total is None else total + term
            out_ref[0, :, columns] = total

    pl.when(lower_heads)(lambda: add(near_a))
    pl.when(jnp.logical_not(lower_heads))(lambda: add(near_b))
    levels = (zero_ref[0], far_ref[0, 0], far_ref[1, 0])
    out_ref[0] = far_product(levels, 0, turned_ref, lw_ref, place, out_ref[0], stack)


def end_attended_kernel(place, turned_ref, lw_ref, total_u, total_l, far_ref, out_ref, stack):
    levels = (far_ref[0, 0], far_ref[1, 0], far_ref[2, 0])
    total = jnp.concatenate([total_u[0], total_l[0]], axis=0)
    total = far_product(levels, 3, turned_ref, lw_ref, place, total, stack)
    out_ref[...] = total.astype(BF).T


def begin_attended(place, turned, weights, values, near, zero, far, *after):
    def head(s, p):
        return lax.rem(2 * p[0] + s, NH)

    def pair(lower):
        def block(s, p):
            reads = (p[0] == 0) == (s < 2) if lower else (p[0] == 0) != (s < 2)
            idle = jnp.where(s < 2, 0, 1)
            return (jnp.where(reads, lax.rem(s, 2), idle), 0, 0, 0)

        return pl.BlockSpec((1, 5, BLK, BLK), block)

    return pl.pallas_call(
        begin_attended_kernel,
        grid_spec=pltpu.PrefetchScalarGridSpec(
            num_scalar_prefetch=1,
            grid=(NH,),
            in_specs=[
                pl.BlockSpec((1, HW, TOK), lambda s, p: (head(s, p), 0, 0)),
                LEVELS,
                pl.BlockSpec((HW, TOK), lambda s, p: (head(s, p), 0)),
                pair(True),
                pair(True),
                pair(False),
                pair(False),
                pl.BlockSpec((1, HW, HW), lambda s, p: (s, 0, 0)),
                pl.BlockSpec((2, 1, HW, HW), lambda s, p: (0, s, 0, 0)),
            ]
            + [ANY] * len(after),
            out_specs=pl.BlockSpec((1, HW, TOK), lambda s, p: (s, 0, 0)),
            scratch_shapes=[pltpu.VMEM((3 * HW, HW), BF)],
        ),
        out_shape=pltpu.HBM((NH, HW, TOK), F32),
        compiler_params=params(),
        cost_estimate=cost(0.3),
        name="begin_attended",
    )(
        place,
        *streamed(turned),
        weights,
        *streamed(values, *near),
        zero,
        far,
        *after,
    )


def end_attended(place, turned, weights, total, far):
    def head(s, p):
        return lax.rem(2 * p[0] + s, NH)

    return pl.pallas_call(
        end_attended_kernel,
        grid_spec=pltpu.PrefetchScalarGridSpec(
            num_scalar_prefetch=1,
            grid=(NH,),
            in_specs=[
                pl.BlockSpec((1, HW, TOK), lambda s, p: (head(s, p), 0, 0)),
                LEVELS,
                pl.BlockSpec((1, HW // 2, TOK), lambda s, p: (s, 0, 0)),
                pl.BlockSpec((1, HW // 2, TOK), lambda s, p: (s, 1, 0)),
                pl.BlockSpec((3, 1, HW, HW), lambda s, p: (0, s, 0, 0)),
            ],
            out_specs=pl.BlockSpec((TOK, HW), lambda s, p: (0, head(s, p))),
            scratch_shapes=[pltpu.VMEM((3 * HW, HW), BF)],
        ),
        out_shape=jax.ShapeDtypeStruct((TOK, NH * HW), BF),
        compiler_params=params(),
        cost_estimate=cost(0.3),
        name="end_attended",
    )(place, *streamed(turned), weights, *streamed(total, total), far)


def behind(value, *made):
    return lax.optimization_barrier((value, *made))[0]


def both(mine):
    return jnp.concatenate([mine, swap(mine, "core", 1, 2)], axis=1)


def local(hidden_in, value_weight, queries, keys, level_weights, out_grad):
    z, x, core, me = (lax.axis_index(a) for a in ("z", "x", "core", "head"))
    place = jnp.stack([core, me, x]).astype(jnp.int32)

    first, send, keep, turned_queries = query_states(place, queries, out_grad, level_weights)
    send_got = swap(send, "core", 1, 2)

    pairs = keep + send_got
    message = pairs[2:].astype(BF)

    (own,) = turned(hidden_in, BLK, 1, "turn_features", message)
    left = shift(own, "head", 1, 4)
    right = shift(own, "head", 3, 4)
    fu = shift(left[:HALF], "head", 1, 4)
    fl = shift(right[HALF:], "head", 3, 4)

    got = swap(message, "z", 1, NZ)
    total = jnp.where(z & 1 == 0, got[0].astype(F32), 0.0)
    level_4, level_5 = pairs[3] + got[1].astype(F32), pairs[4] + got[2].astype(F32)
    message = behind(jnp.stack([level_4, level_5]).astype(BF), own)
    got = swap(message, "z", 2, NZ)
    first_got = lax.ppermute(first, "core", [(1, 0)])
    back_a, *near_a = near(0, keys, turned_queries, out_grad, level_weights, message)
    (turned_weight,) = turned(value_weight, PART, 1, "turn_weight", message)
    total = total + jnp.where(z & 2 == 0, got[0].astype(F32), 0.0)
    message = behind((level_5 + got[1].astype(F32)).astype(BF), back_a, turned_weight)
    got = lax.ppermute(message, "z", [(i + 4, i) for i in range(4)])
    back_b, *near_b = near(2, keys, turned_queries, out_grad, level_weights, message)
    total = total + behind(got, back_b, left, right).astype(F32)
    summed = total
    for distance in (1, 3, 2):
        to = (x + distance) % NX
        level = jnp.where(to ^ x == 1, pairs[0], pairs[1])
        message = (total + jnp.where(to < x, level, 0.0)).astype(BF)
        summed = summed + shift(message, "x", distance, NX).astype(F32)
    begun = begin_values(place, (own, left, right), turned_weight, message)
    values, state = end_values(place, begun, (fu, fl), turned_weight, keys, message)
    other = swap(summed, "core", 1, 2)
    mine = (summed + first_got[:2]).astype(BF)
    other = (other + first_got[2:]).astype(BF)

    got = swap(state, "core", 1, 2)
    zero = jnp.where(core == 1, got, 0.0).astype(BF)
    pair = state[2:] + got[:2]
    message = pair.astype(BF)
    parts = (own, left, right, fu, fl)
    send, keep = weight_terms(place, (back_a, back_b), keys, mine, other, parts, message)
    send_got = swap(send, "core", 1, 2)

    by_one, by_two, by_three = (shift(message, "x", d, NX).astype(F32) for d in (1, 2, 3))
    level_1 = jnp.where(x & 1 == 1, by_one, 0.0)
    level_2 = jnp.where(x == 2, by_one + by_two, jnp.where(x == 3, by_two + by_three, 0.0))
    running = pair + by_one + by_two + by_three
    rows, *messages = pair_sums(place, keep, send_got)
    message = behind(running.astype(BF), rows)
    first, second, third = (shift(messages[d - 1], "x", d, NX) for d in (1, 3, 2))
    rows = rows + first.astype(F32) + second.astype(F32) + third.astype(F32)
    lower_levels = both(jnp.stack([level_1, level_2]).astype(BF))
    begun = begin_attended(
        place, turned_queries, level_weights, values, (*near_a, *near_b), zero, lower_levels, message
    )
    got = swap(message, "z", 1, NZ).astype(F32)
    level_3 = jnp.where(z & 1 == 1, got, 0.0)
    running = running + got
    rows = rows.astype(BF)
    message = behind(running.astype(BF), begun, first)
    got = swap(message, "z", 2, NZ).astype(F32)
    level_4 = jnp.where(z & 2 == 2, got, 0.0)
    running = running + got
    message = running.astype(BF)
    level_5 = lax.ppermute(message, "z", [(i, i + 4) for i in range(4)])
    rows = lax.all_to_all(rows, "z", 0, 0, tiled=True)
    weight_grad = rows.astype(F32).sum(axis=0)
    upper_levels = jnp.stack([level_3.astype(BF), level_4.astype(BF), level_5])
    upper_levels = behind(upper_levels, rows)
    attended = end_attended(place, turned_queries, level_weights, begun, both(upper_levels))
    return attended, weight_grad


def solution(mesh):
    fine = Mesh(mesh.devices.reshape(NZ, NX, 2, 4), ("z", "x", "core", "head"))
    seq = ("z", "x", "core")
    return jax.shard_map(
        local,
        mesh=fine,
        in_specs=(
            P(seq, "head"),
            P(None, "head"),
            P(seq, "head"),
            P(seq, "head"),
            P(None, "head", seq),
            P(seq, "head"),
        ),
        out_specs=(P(seq, "head"), P(seq, "head")),
        check_vma=False,
    )
```

```python
import functools

import jax
import jax.numpy as jnp
from jax import lax
from jax.experimental import pallas as pl
from jax.experimental.pallas import tpu as pltpu
from jax.sharding import Mesh, PartitionSpec as P

BF = jnp.bfloat16
F32 = jnp.float32
HW = 128
NH = 4
TOK = 1024
BLK = 256
DEPTH = 10
FAR = 6
PART = 512
NX, NZ = 4, 8
VMEM = 24 * 1024 * 1024

NT = (((1,), (1,)), ((), ()))
TN = (((0,), (0,)), ((), ()))
NN = (((1,), (0,)), ((), ()))


def dot(a, b, dims=NN):
    return lax.dot_general(a, b, dims, preferred_element_type=F32)


def shift(value, axis, distance, size):
    return lax.ppermute(value, axis, [(i, (i + distance) % size) for i in range(size)])


def swap(value, axis, distance, size):
    return lax.ppermute(value, axis, [(i, i ^ distance) for i in range(size)])


def rows_of(lw_ref, first, count, head):
    rows = []
    for level in range(first, first + count):
        every = lw_ref[level].astype(F32)
        index = lax.broadcasted_iota(jnp.int32, every.shape, 0)
        rows.append(jnp.sum(jnp.where(index == head, every, 0.0), axis=0, keepdims=True))
    return rows


def whole(*shape):
    return pl.BlockSpec(shape, lambda *_: (0,) * len(shape))


LEVELS = whole(DEPTH + 1 + FAR, NH, TOK)


def params():
    return pltpu.CompilerParams(
        dimension_semantics=("arbitrary",), vmem_limit_bytes=VMEM
    )


def cost(us):
    return pl.CostEstimate(flops=int(us * 1.15e9), bytes_accessed=1000, transcendentals=0)


ANY = pl.BlockSpec(memory_space=pl.ANY)


def streamed(*values):
    return [pltpu.with_memory_space_constraint(value, pltpu.HBM) for value in values]


def turn_kernel(in_ref, *rest):
    turned = in_ref[...].T
    at = 0
    for out_ref in rest[1:]:
        out_ref[...] = turned[at : at + out_ref.shape[0], :]
        at += out_ref.shape[0]


def turned(value, side, count, name, after):
    rows, columns = value.shape
    part = columns // count
    return pl.pallas_call(
        turn_kernel,
        grid=(rows // side,),
        in_specs=[pl.BlockSpec((side, columns), lambda i: (i, 0)), ANY],
        out_specs=[pl.BlockSpec((part, side), lambda i: (0, i))] * count,
        out_shape=[jax.ShapeDtypeStruct((part, rows), value.dtype)] * count,
        compiler_params=params(),
        cost_estimate=cost(1.5),
        name=name,
    )(value, after)


def query_state_kernel(place, q_u, q_l, g_u, g_l, lw_ref, *rest):
    first_ref, send_ref, keep_ref, turned_ref, stack = rest[-5:]
    slot = pl.program_id(0)
    half = TOK // 2
    turned_ref[0, :, :half] = q_u[...].T
    turned_ref[0, :, half:] = q_l[...].T
    turned = turned_ref[0]
    head = lax.rem(2 * (1 - place[0]) + slot, NH)
    for digit, row in enumerate(rows_of(lw_ref, DEPTH + 1, FAR, head)):
        stack[digit * HW : (digit + 1) * HW, :] = turned * row.astype(BF)
    state = dot(stack[:, :half], g_u[...]) + dot(stack[:, half:], g_l[...])
    first_ref[0] = state[:HW]
    rest = state[HW:].reshape(FAR - 1, HW, HW)

    @pl.when(slot < 2)
    def _():
        send_ref[:, 0] = rest

    @pl.when(slot >= 2)
    def _():
        keep_ref[:, 0] = rest


def query_states(place, queries, out_grad, weights, *after):
    def head(s, place):
        return lax.rem(2 * (1 - place[0]) + s, NH)

    return pl.pallas_call(
        query_state_kernel,
        grid_spec=pltpu.PrefetchScalarGridSpec(
            num_scalar_prefetch=1,
            grid=(NH,),
            in_specs=[
                pl.BlockSpec((TOK // 2, HW), lambda s, p: (0, head(s, p))),
                pl.BlockSpec((TOK // 2, HW), lambda s, p: (1, head(s, p))),
                pl.BlockSpec((TOK // 2, HW), lambda s, p: (0, head(s, p))),
                pl.BlockSpec((TOK // 2, HW), lambda s, p: (1, head(s, p))),
                LEVELS,
            ]
            + [ANY] * len(after),
            out_specs=[
                pl.BlockSpec((1, HW, HW), lambda s, p: (s, 0, 0)),
                pl.BlockSpec((FAR - 1, 1, HW, HW), lambda s, p: (0, jnp.minimum(s, 1), 0, 0)),
                pl.BlockSpec((FAR - 1, 1, HW, HW), lambda s, p: (0, jnp.maximum(s - 2, 0), 0, 0)),
                pl.BlockSpec((1, HW, TOK), lambda s, p: (head(s, p), 0, 0)),
            ],
            scratch_shapes=[pltpu.VMEM((FAR * HW, TOK), BF)],
        ),
        out_shape=[
            jax.ShapeDtypeStruct((NH, HW, HW), F32),
            jax.ShapeDtypeStruct((FAR - 1, 2, HW, HW), F32),
            jax.ShapeDtypeStruct((FAR - 1, 2, HW, HW), F32),
            pltpu.HBM((NH, HW, TOK), BF),
        ],
        compiler_params=params(),
        cost_estimate=cost(4),
        name="query_states",
    )(place, *streamed(queries, queries, out_grad, out_grad, weights), *after)


SIDES = TOK // BLK
SQUARES = [(low, high) for low in range(SIDES) for high in range(low, SIDES)]


def diagonal(levels, start, differ, causal):
    columns = slice(start, start + HW)
    weight = jnp.broadcast_to(levels[0][:, columns], (HW, HW))
    for level in range(1, HW.bit_length()):
        weight = jnp.where(differ >= 1 << (level - 1), levels[level][:, columns], weight)
    return jnp.where(causal, weight, 0.0)


def near_kernel(base, k_ref, turned_ref, g_ref, lw_ref, *rest):
    back_ref, *near_refs = rest[-3:]
    levels = rows_of(lw_ref, 0, DEPTH + 1, base + pl.program_id(0))
    earlier = lax.broadcasted_iota(jnp.int32, (HW, HW), 0)
    later = lax.broadcasted_iota(jnp.int32, (HW, HW), 1)
    differ, causal = earlier ^ later, earlier <= later
    zero = jnp.zeros((HW, HW), BF)
    middle = HW.bit_length()
    total = None
    for index, (low, high) in enumerate(SQUARES):
        columns = slice(high * BLK, (high + 1) * BLK)
        scores = dot(k_ref[low * BLK : (low + 1) * BLK, :], turned_ref[0, :, columns])
        if low != high:
            level = BLK.bit_length() + (high ^ low).bit_length() - 1
            square = (scores * levels[level][:, columns]).astype(BF)
        else:
            start = high * BLK
            across = levels[middle][:, start + HW : start + BLK]
            upper = scores[:HW, :HW] * diagonal(levels, start, differ, causal)
            lower = scores[HW:, HW:] * diagonal(levels, start + HW, differ, causal)
            top = jnp.concatenate([upper, scores[:HW, HW:] * across], axis=1).astype(BF)
            square = jnp.concatenate(
                [top, jnp.concatenate([zero, lower.astype(BF)], axis=1)], axis=0
            )
        near_refs[index // 5][0, index % 5] = square
        term = dot(square, g_ref[columns, :])
        total = term if low == high else total + term
        if high == SIDES - 1:
            back_ref[low * BLK : (low + 1) * BLK, :] = total


def near(base, keys, turned, out_grad, weights, *after):
    head = pl.BlockSpec((TOK, HW), lambda h: (0, base + h))
    return pl.pallas_call(
        functools.partial(near_kernel, base),
        grid=(2,),
        in_specs=[head, pl.BlockSpec((1, HW, TOK), lambda h: (base + h, 0, 0)), head, LEVELS]
        + [ANY] * len(after),
        out_specs=[
            pl.BlockSpec((TOK, HW), lambda h: (0, h)),
            pl.BlockSpec((1, 5, BLK, BLK), lambda h: (h, 0, 0, 0)),
            pl.BlockSpec((1, 5, BLK, BLK), lambda h: (h, 0, 0, 0)),
        ],
        out_shape=[
            jax.ShapeDtypeStruct((TOK, 2 * HW), F32),
            pltpu.HBM((2, 5, BLK, BLK), BF),
            pltpu.HBM((2, 5, BLK, BLK), BF),
        ],
        compiler_params=params(),
        cost_estimate=cost(3.2),
        name="near",
    )(keys, *streamed(turned), out_grad, weights, *after)


HALF = PART // 2


def begin_values_kernel(place, own, left, right, w_ref, *rest):
    me = place[1]
    total = None
    for distance, part in ((0, own), (3, left), (1, right)):
        at = pl.multiple_of(lax.rem(me + distance, 4) * PART, PART)
        term = dot(w_ref[:, pl.ds(at, PART)], part[...])
        total = term if total is None else total + term
    rest[-1][...] = total


def end_values_kernel(place, total_ref, fu, fl, w_upper, w_lower, k_ref, *rest):
    v_ref, state_ref = rest[-2:]
    tile = pl.program_id(0)
    core = place[0]
    far = dot(w_upper[...], fu[...]) + dot(w_lower[...], fl[...])
    v_ref[...] = (total_ref[...] + far).astype(BF)

    @pl.when(tile == 0)
    def _():
        state_ref[...] = jnp.zeros_like(state_ref)

    for slot in range(NH):
        at = pl.multiple_of(lax.rem(2 * (1 - core) + slot, NH) * HW, HW)
        state_ref[slot] += dot(v_ref[pl.ds(at, HW), :], k_ref[:, pl.ds(at, HW)])


def begin_values(place, parts, turned_weight, *after):
    wide = pl.BlockSpec((PART, BLK), lambda i, p: (0, i))
    return pl.pallas_call(
        begin_values_kernel,
        grid_spec=pltpu.PrefetchScalarGridSpec(
            num_scalar_prefetch=1,
            grid=(TOK // BLK,),
            in_specs=[wide] * 3 + [whole(NH * HW, 4 * PART)] + [ANY] * len(after),
            out_specs=wide,
        ),
        out_shape=jax.ShapeDtypeStruct((NH * HW, TOK), F32),
        compiler_params=params(),
        cost_estimate=cost(3.5),
        name="begin_values",
    )(place, *parts, turned_weight, *after)


def end_values(place, total, parts, turned_weight, keys, *after):
    tile = pl.BlockSpec((HALF, BLK), lambda i, p: (0, i))
    wide = pl.BlockSpec((PART, BLK), lambda i, p: (0, i))

    def weight(offset):
        return pl.BlockSpec((NH * HW, HALF), lambda i, p: (0, lax.rem(p[1] + 2, 4) * 2 + offset))

    return pl.pallas_call(
        end_values_kernel,
        grid_spec=pltpu.PrefetchScalarGridSpec(
            num_scalar_prefetch=1,
            grid=(TOK // BLK,),
            in_specs=[
                wide,
                tile,
                tile,
                weight(0),
                weight(1),
                pl.BlockSpec((BLK, NH * HW), lambda i, p: (i, 0)),
            ]
            + [ANY] * len(after),
            out_specs=[wide, pl.BlockSpec((NH, HW, HW), lambda i, p: (0, 0, 0))],
        ),
        out_shape=[
            pltpu.HBM((NH * HW, TOK), BF),
            jax.ShapeDtypeStruct((NH, HW, HW), F32),
        ],
        compiler_params=params(),
        cost_estimate=cost(3.7),
        name="end_values",
    )(place, total, *parts, turned_weight, turned_weight, keys, *after)


def share_out(place, term, plane, send_ref, keep_ref):
    core, col = place[0], place[2]
    for x in range(NX):
        turn = lax.rem(x - col + NX, NX)
        theirs = pl.multiple_of(x * 64 + (1 - core) * 32, 32)
        ours = pl.multiple_of(x * 64 + core * 32, 32)
        send_ref[turn, plane] = term[pl.ds(theirs, 32), :]
        keep_ref[turn, plane] = term[pl.ds(ours, 32), :]


def distance_of(step):
    return jnp.where(step == 0, 0, jnp.where(step == 1, 3, jnp.where(step == 2, 1, 2)))


def terms_kernel(place, near_a, near_b, k_ref, mine_ref, other_ref, *rest):
    own, left, right, fu, fl = rest[:5]
    send_ref, keep_ref, grad, term = rest[-4:]
    core = place[0]
    step = pl.program_id(0)

    @pl.when(step == 0)
    def _():
        for slot in range(NH):
            at = pl.multiple_of(lax.rem(2 * core + slot, NH) * HW, HW)
            state = mine_ref[slot] if slot < 2 else other_ref[slot - 2]
            far = dot(k_ref[:, pl.ds(at, HW)], state)
            columns = slice(slot % 2 * HW, (slot % 2 + 1) * HW)
            lower_heads = (core == 0) == (slot < 2)
            near = jnp.where(lower_heads, near_a[:, columns], near_b[:, columns])
            grad[:, pl.ds(at, HW)] = (near + far).astype(BF)

    halves = [(part.at[:HALF, :], part.at[HALF:, :]) for part in (own, left, right)]
    for index, pair in enumerate((*halves, (fu, fl))):

        @pl.when(step == index)
        def _(pair=pair):
            for plane in range(2):
                term[plane] = dot(pair[plane][...], grad[...])
                share_out(place, term.at[plane], plane, send_ref, keep_ref)


def shares():
    return pl.BlockSpec(
        (NX, 2, 32, NH * HW), lambda i, p: (0, lax.rem(p[1] + distance_of(i), 4), 0, 0)
    )


def weight_terms(place, near, keys, mine, other, parts, *after):
    return pl.pallas_call(
        terms_kernel,
        grid_spec=pltpu.PrefetchScalarGridSpec(
            num_scalar_prefetch=1,
            grid=(4,),
            in_specs=[
                whole(TOK, 2 * HW),
                whole(TOK, 2 * HW),
                whole(TOK, NH * HW),
                whole(2, HW, HW),
                whole(2, HW, HW),
            ]
            + [whole(PART, TOK)] * 3
            + [whole(HALF, TOK)] * 2
            + [ANY] * len(after),
            out_specs=[shares(), shares()],
            scratch_shapes=[
                pltpu.VMEM((TOK, NH * HW), BF),
                pltpu.VMEM((2, HALF, NH * HW), F32),
            ],
        ),
        out_shape=[
            jax.ShapeDtypeStruct((NX, NZ, 32, NH * HW), F32),
            pltpu.HBM((NX, NZ, 32, NH * HW), F32),
        ],
        compiler_params=params(),
        cost_estimate=cost(5),
        name="weight_terms",
    )(place, *near, keys, mine, other, *parts, *after)


def pair_kernel(place, kept_u, kept_l, got, own_ref, *messages):
    for plane, kept in enumerate((kept_u, kept_l)):
        own_ref[plane] = kept[0, 0] + got[0, plane]
        for turn in range(1, NX):
            messages[turn - 1][plane] = (kept[turn, 0] + got[turn, plane]).astype(BF)


def pair_sums(place, kept, got):
    def plane(offset):
        return pl.BlockSpec(
            (NX, 1, 32, NH * HW),
            lambda i, p: (0, 2 * lax.rem(p[1] + distance_of(i), 4) + offset, 0, 0),
        )

    return pl.pallas_call(
        pair_kernel,
        grid_spec=pltpu.PrefetchScalarGridSpec(
            num_scalar_prefetch=1,
            grid=(4,),
            in_specs=[plane(0), plane(1), shares()],
            out_specs=[
                pl.BlockSpec((2, 32, NH * HW), lambda i, p: (lax.rem(p[1] + distance_of(i), 4), 0, 0))
            ]
            * 4,
        ),
        out_shape=[jax.ShapeDtypeStruct((NZ, 32, NH * HW), F32)]
        + [jax.ShapeDtypeStruct((NZ, 32, NH * HW), BF)] * 3,
        compiler_params=params(),
        cost_estimate=cost(1.1),
        name="pair_sums",
    )(place, *streamed(kept, kept), got)


def far_product(levels, first, turned_ref, lw_ref, place, total, stack):
    head = lax.rem(2 * place[0] + pl.program_id(0), NH)
    rows = rows_of(lw_ref, DEPTH + 1 + first, 3, head)
    for index, level in enumerate(levels):
        stack[index * HW : (index + 1) * HW, :] = level
    product = dot(stack[...], turned_ref[0])
    for index in range(3):
        total = total + product[index * HW : (index + 1) * HW, :] * rows[index]
    return total


def begin_attended_kernel(place, turned_ref, lw_ref, v_ref, *rest):
    near_a, near_b, zero_ref, far_ref = rest[:2], rest[2:4], rest[4], rest[5]
    out_ref, stack = rest[-2:]
    lower_heads = (place[0] == 0) == (pl.program_id(0) < 2)

    def add(near_refs):
        for high in range(SIDES):
            columns = slice(high * BLK, (high + 1) * BLK)
            total = None
            for index, (low, other) in enumerate(SQUARES):
                if other == high:
                    term = dot(v_ref[:, low * BLK : (low + 1) * BLK], near_refs[index // 5][0, index % 5])
                    total = term if total is None else total + term
            out_ref[0, :, columns] = total

    pl.when(lower_heads)(lambda: add(near_a))
    pl.when(jnp.logical_not(lower_heads))(lambda: add(near_b))
    levels = (zero_ref[0], far_ref[0, 0], far_ref[1, 0])
    out_ref[0] = far_product(levels, 0, turned_ref, lw_ref, place, out_ref[0], stack)


def end_attended_kernel(place, turned_ref, lw_ref, total_u, total_l, far_ref, out_ref, stack):
    levels = (far_ref[0, 0], far_ref[1, 0], far_ref[2, 0])
    total = jnp.concatenate([total_u[0], total_l[0]], axis=0)
    total = far_product(levels, 3, turned_ref, lw_ref, place, total, stack)
    out_ref[...] = total.astype(BF).T


def begin_attended(place, turned, weights, values, near, zero, far, *after):
    def head(s, p):
        return lax.rem(2 * p[0] + s, NH)

    def pair(lower):
        def block(s, p):
            reads = (p[0] == 0) == (s < 2) if lower else (p[0] == 0) != (s < 2)
            idle = jnp.where(s < 2, 0, 1)
            return (jnp.where(reads, lax.rem(s, 2), idle), 0, 0, 0)

        return pl.BlockSpec((1, 5, BLK, BLK), block)

    return pl.pallas_call(
        begin_attended_kernel,
        grid_spec=pltpu.PrefetchScalarGridSpec(
            num_scalar_prefetch=1,
            grid=(NH,),
            in_specs=[
                pl.BlockSpec((1, HW, TOK), lambda s, p: (head(s, p), 0, 0)),
                LEVELS,
                pl.BlockSpec((HW, TOK), lambda s, p: (head(s, p), 0)),
                pair(True),
                pair(True),
                pair(False),
                pair(False),
                pl.BlockSpec((1, HW, HW), lambda s, p: (s, 0, 0)),
                pl.BlockSpec((2, 1, HW, HW), lambda s, p: (0, s, 0, 0)),
            ]
            + [ANY] * len(after),
            out_specs=pl.BlockSpec((1, HW, TOK), lambda s, p: (s, 0, 0)),
            scratch_shapes=[pltpu.VMEM((3 * HW, HW), BF)],
        ),
        out_shape=pltpu.HBM((NH, HW, TOK), F32),
        compiler_params=params(),
        cost_estimate=cost(0.3),
        name="begin_attended",
    )(
        place,
        *streamed(turned),
        weights,
        *streamed(values, *near),
        zero,
        far,
        *after,
    )


def end_attended(place, turned, weights, total, far):
    def head(s, p):
        return lax.rem(2 * p[0] + s, NH)

    return pl.pallas_call(
        end_attended_kernel,
        grid_spec=pltpu.PrefetchScalarGridSpec(
            num_scalar_prefetch=1,
            grid=(NH,),
            in_specs=[
                pl.BlockSpec((1, HW, TOK), lambda s, p: (head(s, p), 0, 0)),
                LEVELS,
                pl.BlockSpec((1, HW // 2, TOK), lambda s, p: (s, 0, 0)),
                pl.BlockSpec((1, HW // 2, TOK), lambda s, p: (s, 1, 0)),
                pl.BlockSpec((3, 1, HW, HW), lambda s, p: (0, s, 0, 0)),
            ],
            out_specs=pl.BlockSpec((TOK, HW), lambda s, p: (0, head(s, p))),
            scratch_shapes=[pltpu.VMEM((3 * HW, HW), BF)],
        ),
        out_shape=jax.ShapeDtypeStruct((TOK, NH * HW), BF),
        compiler_params=params(),
        cost_estimate=cost(0.3),
        name="end_attended",
    )(place, *streamed(turned), weights, *streamed(total, total), far)


def behind(value, *made):
    return lax.optimization_barrier((value, *made))[0]


def both(mine):
    return jnp.concatenate([mine, swap(mine, "core", 1, 2)], axis=1)


def local(hidden_in, value_weight, queries, keys, level_weights, out_grad):
    z, x, core, me = (lax.axis_index(a) for a in ("z", "x", "core", "head"))
    place = jnp.stack([core, me, x]).astype(jnp.int32)

    first, send, keep, turned_queries = query_states(place, queries, out_grad, level_weights)
    send_got = swap(send, "core", 1, 2)

    pairs = keep + send_got
    message = pairs[2:].astype(BF)

    (own,) = turned(hidden_in, BLK, 1, "turn_features", message)
    left = shift(own, "head", 1, 4)
    right = shift(own, "head", 3, 4)
    fu = shift(left[:HALF], "head", 1, 4)
    fl = shift(right[HALF:], "head", 3, 4)

    got = swap(message, "z", 1, NZ)
    total = jnp.where(z & 1 == 0, got[0].astype(F32), 0.0)
    level_4, level_5 = pairs[3] + got[1].astype(F32), pairs[4] + got[2].astype(F32)
    message = behind(jnp.stack([level_4, level_5]).astype(BF), own)
    got = swap(message, "z", 2, NZ)
    first_got = lax.ppermute(first, "core", [(1, 0)])
    back_a, *near_a = near(0, keys, turned_queries, out_grad, level_weights, message)
    (turned_weight,) = turned(value_weight, PART, 1, "turn_weight", message)
    total = total + jnp.where(z & 2 == 0, got[0].astype(F32), 0.0)
    message = behind((level_5 + got[1].astype(F32)).astype(BF), back_a, turned_weight)
    got = lax.ppermute(message, "z", [(i + 4, i) for i in range(4)])
    back_b, *near_b = near(2, keys, turned_queries, out_grad, level_weights, message)
    total = total + behind(got, back_b, left, right).astype(F32)
    summed = total
    for distance in (1, 3, 2):
        to = (x + distance) % NX
        level = jnp.where(to ^ x == 1, pairs[0], pairs[1])
        message = (total + jnp.where(to < x, level, 0.0)).astype(BF)
        summed = summed + shift(message, "x", distance, NX).astype(F32)
    begun = begin_values(place, (own, left, right), turned_weight, message)
    values, state = end_values(place, begun, (fu, fl), turned_weight, keys, message)
    other = swap(behind(summed, state), "core", 1, 2)
    mine = (summed + first_got[:2]).astype(BF)
    other = (other + first_got[2:]).astype(BF)

    got = swap(state, "core", 1, 2)
    zero = jnp.where(core == 1, got, 0.0).astype(BF)
    pair = state[2:] + got[:2]
    message = pair.astype(BF)
    parts = (own, left, right, fu, fl)
    send, keep = weight_terms(place, (back_a, back_b), keys, mine, other, parts, message)
    send_got = swap(send, "core", 1, 2)

    by_one, by_two, by_three = (shift(message, "x", d, NX).astype(F32) for d in (1, 2, 3))
    level_1 = jnp.where(x & 1 == 1, by_one, 0.0)
    level_2 = jnp.where(x == 2, by_one + by_two, jnp.where(x == 3, by_two + by_three, 0.0))
    running = pair + by_one + by_two + by_three
    rows, *messages = pair_sums(place, keep, send_got)
    message = behind(running.astype(BF), rows)
    first, second, third = (shift(messages[d - 1], "x", d, NX) for d in (1, 3, 2))
    rows = rows + first.astype(F32) + second.astype(F32) + third.astype(F32)
    got = swap(message, "z", 1, NZ).astype(F32)
    level_3 = jnp.where(z & 1 == 1, got, 0.0)
    running = running + got
    lower_levels = both(jnp.stack([level_1, level_2]).astype(BF))
    message = behind(running.astype(BF), first)
    got = swap(message, "z", 2, NZ).astype(F32)
    begun = begin_attended(
        place, turned_queries, level_weights, values, (*near_a, *near_b), zero, lower_levels, message
    )
    level_4 = jnp.where(z & 2 == 2, got, 0.0)
    running = running + got
    rows = rows.astype(BF)
    message = behind(running.astype(BF), begun)
    level_5 = lax.ppermute(message, "z", [(i, i + 4) for i in range(4)])
    rows = lax.all_to_all(rows, "z", 0, 0, tiled=True)
    weight_grad = rows.astype(F32).sum(axis=0)
    upper_levels = jnp.stack([level_3.astype(BF), level_4.astype(BF), level_5])
    attended = end_attended(place, turned_queries, level_weights, begun, both(upper_levels))
    return attended, weight_grad


def solution(mesh):
    fine = Mesh(mesh.devices.reshape(NZ, NX, 2, 4), ("z", "x", "core", "head"))
    seq = ("z", "x", "core")
    return jax.shard_map(
        local,
        mesh=fine,
        in_specs=(
            P(seq, "head"),
            P(None, "head"),
            P(seq, "head"),
            P(seq, "head"),
            P(None, "head", seq),
            P(seq, "head"),
        ),
        out_specs=(P(seq, "head"), P(seq, "head")),
        check_vma=False,
    )
```
